32 devices in a mesh: space: 8 (over y, x, core), species: 4 (over z).
Axes of the slice: x: 2, y: 2, z: 4, core: 2. Of those that a mesh axis runs over, the one named last changes fastest.
Arguments:
- biomass: bfloat16 [512, 16, 1024], P('species', 'space'), may hold values from 0.019897461 to 1
- resources: float32 [128, 16, 1024], P('species', 'space'), may hold values from 0.1 to 4
- capacity: float32 [512, 128], P('species'), may hold values from 0.002 to 0.05
- affinity: float32 [512, 128], P('species'), may hold values from 0.2 to 5
- secretion: bfloat16 [128, 512], P(None, 'species'), may hold values from 0 to 0.059814453
- energy_yield: float32 [128], replicated, may hold values from 0.5 to 2
- maintenance: float32 [512], P('species'), may hold values from 0.3 to 3
- motility: float32 [512], P('species'), may hold values from 0.04 to 0.6
- diffusivity: float32 [128], P('species'), may hold values from 0.02 to 0.6
- supply: float32 [128], P('species'), may hold values from 0.4 to 4
Outputs:
- growth: float32 [512, 16, 1024], P('species', 'space')
- new_biomass: float32 [512, 16, 1024], P('species', 'space')
- new_resources: float32 [128, 16, 1024], P('species', 'space')
The draws below stay inside these ranges and needn't reach their ends.
All inputs are finite; a program needn't handle non-finite values.
Results may differ from the reference program's by a relative error of at most 0.0003.
Values may be sent and summed in bfloat16 or wider, within the bound.
No kernel may reach another device: no remote copies, remote signals or barrier semaphores. Data moves between devices by JAX's collectives and lax.ppermute only.
A program may use at most 64 MiB of HBM per device.

```python
import math
import jax
import jax.numpy as jnp
from jax import lax

STRAINS = 512
RESOURCES = 128
NY = 16
NZ = 64
NX = 16
PLANE = 1024


def levels(key, dims, cuts, smallest, top_value):
    level, own = 1.0, jax.random.fold_in(key, 6)
    for dim, parts in cuts:
        draws = jnp.exp(jax.random.uniform(jax.random.fold_in(own, dim), (parts,), jnp.float32, smallest / len(cuts), top_value / len(cuts)))
        level = level * jnp.repeat(draws, dims[dim] // parts).reshape([-1 if axis == dim else 1 for axis in range(len(dims))])
    return level


def setup_inputs(seed: int = 0) -> dict:
    key_list = jax.random.split(jax.random.key(seed), 11)
    biomass = jnp.clip(jnp.exp(math.log(1.0) - 3.9171631 * jax.random.uniform(key_list[0], (STRAINS, NX, PLANE), jnp.float32) ** levels(key_list[0], (STRAINS, NX, PLANE), ((0, 4), (1, 8)), -0.2, 0.2)), 0.019897461, 1.0).astype(jnp.bfloat16)
    resources = jnp.clip(jnp.exp(math.log(4.0) - 3.6888794 * jax.random.uniform(key_list[1], (RESOURCES, NX, PLANE), jnp.float32) ** levels(key_list[1], (RESOURCES, NX, PLANE), ((0, 4), (1, 8)), -0.2, 0.2)), 0.1, 4.0)
    capacity = jnp.clip(jnp.exp(math.log(0.05) - 3.218876 * jax.random.uniform(key_list[2], (STRAINS, RESOURCES), jnp.float32) ** levels(key_list[2], (STRAINS, RESOURCES), ((0, 4),), -0.2, 0.2)), 0.002, 0.05)
    affinity = jnp.clip(jnp.exp(math.log(5.0) - 3.218876 * jax.random.uniform(key_list[3], (STRAINS, RESOURCES), jnp.float32) ** levels(key_list[3], (STRAINS, RESOURCES), ((0, 4),), -0.2, 0.2)), 0.2, 5.0)
    secretion = jnp.clip(0.059814453 * jax.random.uniform(key_list[4], (RESOURCES, STRAINS), jnp.float32) ** levels(key_list[4], (RESOURCES, STRAINS), ((1, 4),), -0.2, 0.2), 0.0, 0.059814453).astype(jnp.bfloat16)
    energy_yield = jnp.clip(jnp.exp(jax.random.uniform(key_list[5], (RESOURCES,), jnp.float32, math.log(0.5), math.log(2.0))), 0.5, 2.0)
    maintenance = jnp.clip(jnp.exp(math.log(3.0) - 2.3025851 * jax.random.uniform(key_list[6], (STRAINS,), jnp.float32) ** levels(key_list[6], (STRAINS,), ((0, 4),), -0.2, 0.2)), 0.3, 3.0)
    motility = jnp.clip(jnp.exp(math.log(0.6) - 2.7080503 * jax.random.uniform(key_list[7], (STRAINS,), jnp.float32) ** levels(key_list[7], (STRAINS,), ((0, 4),), -0.2, 0.2)), 0.04, 0.6)
    diffusivity = jnp.clip(jnp.exp(math.log(0.6) - 3.4011974 * jax.random.uniform(key_list[8], (RESOURCES,), jnp.float32) ** levels(key_list[8], (RESOURCES,), ((0, 4),), -0.2, 0.2)), 0.02, 0.6)
    supply = jnp.clip(jnp.exp(math.log(4.0) - 2.3025851 * jax.random.uniform(key_list[9], (RESOURCES,), jnp.float32) ** levels(key_list[9], (RESOURCES,), ((0, 4),), -0.2, 0.2)), 0.4, 4.0)
    return dict(biomass=biomass, resources=resources, capacity=capacity, affinity=affinity, secretion=secretion, energy_yield=energy_yield, maintenance=maintenance, motility=motility, diffusivity=diffusivity, supply=supply)


time_step = 0.25


def laplace(padded, depth_cells, width_cells):
    channel_count = padded.shape[0]
    inner_cells = padded[:, 1:-1, :]
    slab_rows = inner_cells.shape[1]
    block_view = inner_cells.reshape(channel_count, slab_rows, depth_cells, width_cells)
    extended = jnp.pad(block_view, ((0, 0), (0, 0), (1, 1), (1, 1)), mode="edge")
    beside_x = padded[:, 2:, :] + padded[:, :-2, :]
    beside_yz = extended[:, :, 2:, 1:-1] + extended[:, :, :-2, 1:-1] + extended[:, :, 1:-1, 2:] + extended[:, :, 1:-1, :-2]
    return beside_x + beside_yz.reshape(channel_count, slab_rows, -1) - 6.0 * inner_cells


def periodic(field):
    return jnp.concatenate([field[:, -1:, :], field, field[:, :1, :]], axis=1)


def reference(biomass, resources, capacity, affinity, secretion, energy_yield, maintenance, motility, diffusivity, supply):
    seen = lax.optimization_barrier(resources.astype(jnp.bfloat16)).astype(jnp.float32)
    seen_flat = seen.reshape(RESOURCES, -1)
    mass = biomass.astype(jnp.float32)
    mass_flat = mass.reshape(STRAINS, -1)
    cell_count = seen_flat.shape[1]

    def per_strain(carry, item):
        consumed, secreted = carry
        cap_row, aff_row, sec_col, mass_row, maint_value = item
        uptake = cap_row[:, None] * seen_flat / (aff_row[:, None] + seen_flat)
        growth_row = jnp.sum(energy_yield[:, None] * uptake, axis=0) - maint_value
        flux_row = jnp.sum(uptake, axis=0)
        rounded = lax.optimization_barrier((mass_row * flux_row).astype(jnp.bfloat16)).astype(jnp.float32)
        consumed = consumed + mass_row[None, :] * uptake
        secreted = secreted + sec_col.astype(jnp.float32)[:, None] * rounded[None, :]
        return (consumed, secreted), growth_row

    start_sums = (jnp.zeros((RESOURCES, cell_count), jnp.float32), jnp.zeros((RESOURCES, cell_count), jnp.float32))
    (consumed, secreted), growth_rows = lax.scan(per_strain, start_sums, (capacity, affinity, secretion.T, mass_flat, maintenance))
    growth = growth_rows.reshape(biomass.shape)
    spread_mass = motility[:, None, None] * laplace(periodic(mass), NY, NZ)
    new_biomass = mass + time_step * (mass * growth + spread_mass)
    spread_resources = diffusivity[:, None, None] * laplace(periodic(resources), NY, NZ)
    net_release = (secreted - consumed).reshape(resources.shape)
    new_resources = resources + time_step * (spread_resources + net_release + supply[:, None, None])
    return growth, new_biomass, new_resources
```

```python
import functools

import jax
import jax.numpy as jnp
from jax import lax
from jax.experimental import pallas as pl
from jax.experimental.pallas import tpu as pltpu
from jax.sharding import PartitionSpec as P

NY = 16
NZ = 64

time_step = 0.25

bf16 = jnp.bfloat16
f32 = jnp.float32
LANES = 128
GROUP = 16
WIDE = 256


def whole():
    return pl.BlockSpec(memory_space=pltpu.VMEM)


def anywhere():
    return pl.BlockSpec(memory_space=pl.ANY)


def params(limit):
    return pltpu.CompilerParams(vmem_limit_bytes=limit << 20)


def estimate(elements):
    return pl.CostEstimate(flops=40 * elements, bytes_accessed=1 << 20, transcendentals=elements)


def spread_kernel(first_ref, capacity_ref, affinity_ref, yield_ref, slope_ref, level_ref):
    strains, resources = capacity_ref.shape
    shift = lax.rem(2 * resources - first_ref[0] - GROUP * pl.program_id(0), resources)
    shift = lax.rem(shift + resources, resources)
    yields = yield_ref[...]
    for group in range(strains // GROUP):
        rows = pl.ds(group * GROUP, GROUP)
        level = 1.0 / (capacity_ref[rows, :] * yields)
        slope = pltpu.roll(affinity_ref[rows, :] * level, shift, 1)
        level = pltpu.roll(level, shift, 1)
        for r in range(GROUP):
            slope_ref[r, group] = jnp.broadcast_to(slope[:, r : r + 1], (GROUP, LANES))
            level_ref[r, group] = jnp.broadcast_to(level[:, r : r + 1], (GROUP, LANES))


def spread_coefficients(first, capacity, affinity, energy_yield):
    strains, resources = capacity.shape
    groups = strains // GROUP
    shape = jax.ShapeDtypeStruct((resources, groups, GROUP, LANES), f32)
    block = pl.BlockSpec((GROUP, groups, GROUP, LANES), lambda i: (i, 0, 0, 0))
    return pl.pallas_call(
        spread_kernel,
        grid=(resources // GROUP,),
        out_shape=(shape, shape),
        in_specs=[pl.BlockSpec(memory_space=pltpu.SMEM)] + [whole()] * 3,
        out_specs=(block, block),
        compiler_params=params(16),
        cost_estimate=estimate(resources * strains * LANES),
    )(first, capacity, affinity, energy_yield[None, :])


def uptake_sums(row0, seen_refs, slope_hbm, level_hbm, inverse_ref, mass_s, growth_ref, flux_ref,
                consumed_ref, y_s, slope_s, level_s, eaten_s, sem):
    rows, cells = y_s.shape
    groups = mass_s.shape[0] // GROUP
    blocks = rows // GROUP

    def fetch(block, slot):
        part = pl.ds(row0 + block * GROUP, GROUP)
        return (
            pltpu.make_async_copy(slope_hbm.at[part], slope_s.at[slot], sem.at[0, slot]),
            pltpu.make_async_copy(level_hbm.at[part], level_s.at[slot], sem.at[1, slot]),
        )

    for copy in fetch(0, 0):
        copy.start()
    start = 0
    for ref in seen_refs:
        count = ref.shape[0]
        y_s[start : start + count, :] = 1.0 / ref[...].astype(f32)
        start += count

    def per_block(block, _):
        slot = lax.rem(block, 2)
        for copy in fetch(block, slot):
            copy.wait()

        @pl.when(block + 1 < blocks)
        def _():
            for copy in fetch(block + 1, 1 - slot):
                copy.start()

        r0 = pl.multiple_of(block * GROUP, GROUP)

        def per_tile(tile, _):
            lanes = pl.ds(pl.multiple_of(tile * LANES, LANES), LANES)
            y_rows = y_s[pl.ds(r0, GROUP), lanes]
            inverse = inverse_ref[pl.ds(row0 + r0, GROUP), :]
            growth = [growth_ref[g * GROUP : (g + 1) * GROUP, lanes] for g in range(groups)]
            flux = [None] * groups
            for r in range(GROUP):
                y = jnp.broadcast_to(y_rows[r : r + 1], (GROUP, LANES))
                scale = jnp.broadcast_to(inverse[r : r + 1], (GROUP, LANES)).astype(bf16)
                eaten = None
                for g in range(groups):
                    gain = pl.reciprocal(slope_s[slot, r, g] * y + level_s[slot, r, g], approx=True)
                    growth[g] = growth[g] + gain
                    short = gain.astype(bf16)
                    taken = short * scale
                    flux[g] = taken if r == 0 else flux[g] + taken
                    part = short * mass_s[g * GROUP : (g + 1) * GROUP, lanes]
                    eaten = part if g == 0 else eaten + part
                eaten_s[r0 + r, :, lanes] = eaten
            for g in range(groups):
                strains = slice(g * GROUP, (g + 1) * GROUP)
                growth_ref[strains, lanes] = growth[g]
                flux_ref[strains, lanes] += flux[g].astype(f32)
            return 0

        lax.fori_loop(0, cells // LANES, per_tile, 0)
        return 0

    lax.fori_loop(0, blocks, per_block, 0)

    shape = (GROUP, GROUP * GROUP)
    ones = lax.broadcasted_iota(jnp.int32, shape, 1) // GROUP
    ones = (ones == lax.broadcasted_iota(jnp.int32, shape, 0)).astype(f32).astype(bf16)
    for block in range(blocks):
        part = slice(block * GROUP, (block + 1) * GROUP)
        inverse = inverse_ref[row0 + block * GROUP : row0 + (block + 1) * GROUP, :1]
        for tile in range(cells // WIDE):
            lanes = slice(tile * WIDE, (tile + 1) * WIDE)
            sums = jnp.dot(
                ones, eaten_s[part, :, lanes].reshape(GROUP * GROUP, WIDE), preferred_element_type=f32
            )
            consumed_ref[part, lanes] = sums * inverse


def copy_mass(mass_ref, mass_s):
    mass_s[...] = mass_ref[...].astype(f32).astype(bf16)


def first_kernel(row0, parts, *refs):
    seen = refs[:parts]
    slope, level, inverse, mass_ref = refs[parts : parts + 4]
    growth_ref, flux_ref, consumed_ref = refs[parts + 4 : parts + 7]
    y_s, mass_s, slope_s, level_s, eaten_s, sem = refs[parts + 7 :]
    copy_mass(mass_ref, mass_s)
    growth_ref[...] = jnp.zeros_like(growth_ref)
    flux_ref[...] = jnp.zeros_like(flux_ref)
    uptake_sums(row0, seen, slope, level, inverse, mass_s, growth_ref, flux_ref, consumed_ref,
                y_s, slope_s, level_s, eaten_s, sem)


def finish(flux_ref, mass_ref, secretion_ref, consumed_refs, net_refs):
    cells = flux_ref.shape[1]
    for tile in range(cells // WIDE):
        lanes = slice(tile * WIDE, (tile + 1) * WIDE)
        product = (mass_ref[:, lanes].astype(f32) * flux_ref[:, lanes]).astype(bf16)
        secreted = jnp.dot(secretion_ref[...], product, preferred_element_type=f32)
        consumed = [ref[:, lanes] for ref in consumed_refs]
        net = secreted - (consumed[0] if len(consumed) == 1 else jnp.concatenate(consumed, axis=0))
        start = 0
        for ref in net_refs:
            count = ref.shape[0]
            ref[:, lanes] = net[start : start + count].astype(ref.dtype)
            start += count


def second_kernel(row0, parts, owners, *refs):
    seen = refs[:parts]
    slope, level, inverse, mass_ref = refs[parts : parts + 4]
    growth_in, flux_in, consumed_in, secretion_ref = refs[parts + 4 : parts + 8]
    growth_ref = refs[parts + 8]
    net_refs = refs[parts + 9 : parts + 9 + owners]
    flux_s, consumed_s, y_s, mass_s, slope_s, level_s, eaten_s, sem = refs[parts + 9 + owners :]
    copy_mass(mass_ref, mass_s)
    growth_ref[...] = growth_in[...]
    flux_s[...] = flux_in[...]
    uptake_sums(row0, seen, slope, level, inverse, mass_s, growth_ref, flux_s, consumed_s,
                y_s, slope_s, level_s, eaten_s, sem)
    finish(flux_s, mass_ref, secretion_ref, (consumed_in, consumed_s), net_refs)


def only_kernel(row0, parts, owners, *refs):
    seen = refs[:parts]
    slope, level, inverse, mass_ref, secretion_ref = refs[parts : parts + 5]
    growth_ref = refs[parts + 5]
    net_refs = refs[parts + 6 : parts + 6 + owners]
    flux_s, consumed_s, y_s, mass_s, slope_s, level_s, eaten_s, sem = refs[parts + 6 + owners :]
    copy_mass(mass_ref, mass_s)
    growth_ref[...] = jnp.zeros_like(growth_ref)
    flux_s[...] = jnp.zeros_like(flux_s)
    uptake_sums(row0, seen, slope, level, inverse, mass_s, growth_ref, flux_s, consumed_s,
                y_s, slope_s, level_s, eaten_s, sem)
    finish(flux_s, mass_ref, secretion_ref, (consumed_s,), net_refs)


def work_space(rows, strains, cells):
    groups = strains // GROUP
    return [
        pltpu.VMEM((rows, cells), f32),
        pltpu.VMEM((strains, cells), bf16),
        pltpu.VMEM((2, GROUP, groups, GROUP, LANES), f32),
        pltpu.VMEM((2, GROUP, groups, GROUP, LANES), f32),
        pltpu.VMEM((rows, GROUP, cells), bf16),
        pltpu.SemaphoreType.DMA((2, 2)),
    ]


def exchange(own, others, slope, level, inverse, mass, secretion):
    strains, cells = mass.shape
    held = own.shape[0]
    total = inverse.shape[0]
    sums = jax.ShapeDtypeStruct((strains, cells), f32)
    nets = tuple(
        jax.ShapeDtypeStruct((held, cells), f32 if i == 0 else bf16) for i in range(total // held)
    )
    hbm = [anywhere(), anywhere(), whole(), whole()]
    if held % GROUP:
        seen = jnp.concatenate([own] + others, axis=0)
        outs = pl.pallas_call(
            functools.partial(only_kernel, 0, 1, len(nets)),
            out_shape=(sums,) + nets,
            in_specs=[whole()] + hbm + [whole()],
            out_specs=(whole(),) * (1 + len(nets)),
            scratch_shapes=[pltpu.VMEM((strains, cells), f32), pltpu.VMEM((total, cells), f32)]
            + work_space(total, strains, cells),
            compiler_params=params(56),
            cost_estimate=estimate(total * strains * cells),
        )(seen, slope, level, inverse, mass, secretion)
        return outs[0], outs[1:]
    growth, flux, consumed = pl.pallas_call(
        functools.partial(first_kernel, 0, 1),
        out_shape=(sums, sums, jax.ShapeDtypeStruct((held, cells), f32)),
        in_specs=[whole()] + hbm,
        out_specs=(whole(),) * 3,
        scratch_shapes=work_space(held, strains, cells),
        compiler_params=params(40),
        cost_estimate=estimate(held * strains * cells),
    )(own, slope, level, inverse, mass)
    rest = total - held
    outs = pl.pallas_call(
        functools.partial(second_kernel, held, len(others), len(nets)),
        out_shape=(sums,) + nets,
        in_specs=[whole()] * len(others) + hbm + [whole()] * 4,
        out_specs=(whole(),) * (1 + len(nets)),
        scratch_shapes=[pltpu.VMEM((strains, cells), f32), pltpu.VMEM((rest, cells), f32)]
        + work_space(rest, strains, cells),
        compiler_params=params(56),
        cost_estimate=estimate(rest * strains * cells),
    )(*others, slope, level, inverse, mass, growth, flux, consumed, secretion)
    return outs[0], outs[1:]


def laplace(field, low, high, planes, plane):
    cell = lax.broadcasted_iota(jnp.int32, (field[0].shape[0], plane), 1)
    z = lax.rem(cell, NZ)
    out = []
    for x in range(planes):
        v = field[x]
        beside = (low if x == 0 else field[x - 1]) + (high if x == planes - 1 else field[x + 1])
        beside += jnp.where(z == 0, v, pltpu.roll(v, 1, 1))
        beside += jnp.where(z == NZ - 1, v, pltpu.roll(v, plane - 1, 1))
        beside += jnp.where(cell < NZ, v, pltpu.roll(v, NZ, 1))
        beside += jnp.where(cell >= plane - NZ, v, pltpu.roll(v, plane - NZ, 1))
        out.append(beside - 6.0 * v)
    return out


def planes_of(ref, rows, planes, plane):
    return [ref[rows, x * plane : (x + 1) * plane].astype(f32) for x in range(planes)]


def step_kernel(planes, plane, mass_ref, low_ref, high_ref, sum_ref, maintenance_ref, motility_ref,
                growth_ref, new_ref):
    def per_group(group, _):
        rows = pl.ds(pl.multiple_of(group * GROUP, GROUP), GROUP)
        mass = planes_of(mass_ref, rows, planes, plane)
        spread = laplace(mass, low_ref[rows, :].astype(f32), high_ref[rows, :].astype(f32), planes, plane)
        maintenance = maintenance_ref[rows, :1]
        motility = motility_ref[rows, :1]
        for x in range(planes):
            lanes = slice(x * plane, (x + 1) * plane)
            growth = sum_ref[rows, lanes] - maintenance
            growth_ref[rows, lanes] = growth
            new_ref[rows, lanes] = mass[x] + time_step * (mass[x] * growth + motility * spread[x])
        return 0

    lax.fori_loop(0, mass_ref.shape[0] // GROUP, per_group, 0)


def resource_kernel(planes, plane, field_ref, low_ref, high_ref, net_ref, diffusivity_ref, supply_ref,
                    new_ref):
    rows = slice(0, field_ref.shape[0])
    field = planes_of(field_ref, rows, planes, plane)
    spread = laplace(field, low_ref[...], high_ref[...], planes, plane)
    for x in range(planes):
        lanes = slice(x * plane, (x + 1) * plane)
        change = diffusivity_ref[:, :1] * spread[x] + net_ref[:, lanes] + supply_ref[:, :1]
        new_ref[:, lanes] = field[x] + time_step * change


def column(values):
    return jnp.broadcast_to(values[:, None], (values.shape[0], LANES))


def halo(block, axis):
    count = lax.axis_size(axis)
    forward = [(i, (i + 1) % count) for i in range(count)]
    backward = [(target, source) for source, target in forward]
    low = lax.ppermute(block[:, -1, :], axis, forward)
    high = lax.ppermute(block[:, 0, :], axis, backward)
    return low, high


def shifted(value, axis, shift):
    count = lax.axis_size(axis)
    return lax.ppermute(value, axis, [(i, (i + shift) % count) for i in range(count)])


def per_device(
    biomass,
    resources,
    capacity,
    affinity,
    secretion,
    energy_yield,
    maintenance,
    motility,
    diffusivity,
    supply,
):
    strains, slab_rows, plane = biomass.shape
    cells = slab_rows * plane
    held = resources.shape[0]
    count = lax.axis_size("species")
    total = held * count
    mass = biomass.reshape(strains, cells)
    field = resources.reshape(held, cells)
    own = field.astype(bf16)
    others = [shifted(own, "species", -j) for j in range(1, count)]
    first = lax.axis_index("species") * held
    turned = lax.dynamic_slice_in_dim(jnp.concatenate([energy_yield, energy_yield]), first, total)
    inverse = column(1.0 / turned)
    secretion = lax.dynamic_slice_in_dim(jnp.concatenate([secretion, secretion]), first, total, 0)
    slope, level = spread_coefficients(first[None].astype(jnp.int32), capacity, affinity, energy_yield)
    mass_low, mass_high = halo(biomass, "space")
    field_low, field_high = halo(resources, "space")
    gained, nets = exchange(own, others, slope, level, inverse, mass, secretion)
    arrived = [shifted(nets[j], "species", j) for j in range(1, count)]
    sums = jax.ShapeDtypeStruct((strains, cells), f32)
    growth, new_biomass = pl.pallas_call(
        functools.partial(step_kernel, slab_rows, plane),
        out_shape=(sums, sums),
        in_specs=[whole()] * 6,
        out_specs=(whole(),) * 2,
        compiler_params=params(32),
        cost_estimate=estimate(strains * cells * 8),
    )(mass, mass_low, mass_high, gained, column(maintenance), column(motility))
    partial = pl.pallas_call(
        functools.partial(resource_kernel, slab_rows, plane),
        out_shape=jax.ShapeDtypeStruct((held, cells), f32),
        in_specs=[whole()] * 6,
        out_specs=whole(),
        compiler_params=params(32),
        cost_estimate=estimate(held * cells * 8),
    )(field, field_low, field_high, nets[0], column(diffusivity), column(supply))
    received = arrived[0].astype(f32)
    for part in arrived[1:]:
        received = received + part.astype(f32)
    new_resources = partial + time_step * received
    shape = (strains, slab_rows, plane)
    return growth.reshape(shape), new_biomass.reshape(shape), new_resources.reshape(resources.shape)


def solution(mesh):
    return jax.shard_map(
        per_device,
        mesh=mesh,
        in_specs=(
            P("species", "space", None),
            P("species", "space", None),
            P("species", None),
            P("species", None),
            P(None, "species"),
            P(),
            P("species"),
            P("species"),
            P("species"),
            P("species"),
        ),
        out_specs=(
            P("species", "space", None),
            P("species", "space", None),
            P("species", "space", None),
        ),
        check_vma=False,
    )
```

```python
import functools

import jax
import jax.numpy as jnp
from jax import lax
from jax.experimental import pallas as pl
from jax.experimental.pallas import tpu as pltpu
from jax.sharding import PartitionSpec as P

NY = 16
NZ = 64

time_step = 0.25

bf16 = jnp.bfloat16
f32 = jnp.float32
LANES = 128
GROUP = 16
WIDE = 256


def whole():
    return pl.BlockSpec(memory_space=pltpu.VMEM)


def params(limit):
    return pltpu.CompilerParams(vmem_limit_bytes=limit << 20)


def estimate(elements):
    return pl.CostEstimate(flops=40 * elements, bytes_accessed=1 << 20, transcendentals=elements)


def uptake_sums(row0, seen_refs, first_ref, capacity_ref, affinity_ref, yield_ref, inverse_ref, mass_s,
                growth_ref, flux_ref, consumed_ref, y_s, slopes_s, levels_s, slope_s, level_s, eaten_s):
    rows, cells = y_s.shape
    strains, resources = capacity_ref.shape
    groups = strains // GROUP
    blocks = rows // GROUP
    start = 0
    for ref in seen_refs:
        count = ref.shape[0]
        y_s[start : start + count, :] = 1.0 / ref[...].astype(f32)
        start += count
    turn = lax.rem(2 * resources - first_ref[0] - row0, resources)
    level = 1.0 / (capacity_ref[...] * yield_ref[...])
    slopes_s[...] = pltpu.roll(affinity_ref[...] * level, turn, 1)
    levels_s[...] = pltpu.roll(level, turn, 1)

    def per_block(block, _):
        r0 = pl.multiple_of(block * GROUP, GROUP)
        turn = lax.rem(resources - r0, resources)
        members = [pl.ds(g * GROUP, GROUP) for g in range(groups)]
        slopes = [pltpu.roll(slopes_s[m, :], turn, 1) for m in members]
        levels = [pltpu.roll(levels_s[m, :], turn, 1) for m in members]
        for r in range(GROUP):
            for g in range(groups):
                slope_s[r, g] = jnp.broadcast_to(slopes[g][:, r : r + 1], (GROUP, LANES))
                level_s[r, g] = jnp.broadcast_to(levels[g][:, r : r + 1], (GROUP, LANES))

        def per_tile(tile, _):
            lanes = pl.ds(pl.multiple_of(tile * LANES, LANES), LANES)
            y_rows = y_s[pl.ds(r0, GROUP), lanes]
            inverse = inverse_ref[pl.ds(row0 + r0, GROUP), :]
            growth = [growth_ref[g * GROUP : (g + 1) * GROUP, lanes] for g in range(groups)]
            flux = [None] * groups
            for r in range(GROUP):
                y = jnp.broadcast_to(y_rows[r : r + 1], (GROUP, LANES))
                scale = jnp.broadcast_to(inverse[r : r + 1], (GROUP, LANES)).astype(bf16)
                eaten = None
                for g in range(groups):
                    gain = pl.reciprocal(slope_s[r, g] * y + level_s[r, g], approx=True)
                    growth[g] = growth[g] + gain
                    short = gain.astype(bf16)
                    taken = short * scale
                    flux[g] = taken if r == 0 else flux[g] + taken
                    part = short * mass_s[g * GROUP : (g + 1) * GROUP, lanes]
                    eaten = part if g == 0 else eaten + part
                eaten_s[r0 + r, :, lanes] = eaten
            for g in range(groups):
                strains = slice(g * GROUP, (g + 1) * GROUP)
                growth_ref[strains, lanes] = growth[g]
                flux_ref[strains, lanes] += flux[g].astype(f32)
            return 0

        lax.fori_loop(0, cells // LANES, per_tile, 0)
        return 0

    lax.fori_loop(0, blocks, per_block, 0)

    shape = (GROUP, GROUP * GROUP)
    ones = lax.broadcasted_iota(jnp.int32, shape, 1) // GROUP
    ones = (ones == lax.broadcasted_iota(jnp.int32, shape, 0)).astype(f32).astype(bf16)
    for block in range(blocks):
        part = slice(block * GROUP, (block + 1) * GROUP)
        inverse = inverse_ref[row0 + block * GROUP : row0 + (block + 1) * GROUP, :1]
        for tile in range(cells // WIDE):
            lanes = slice(tile * WIDE, (tile + 1) * WIDE)
            sums = jnp.dot(
                ones, eaten_s[part, :, lanes].reshape(GROUP * GROUP, WIDE), preferred_element_type=f32
            )
            consumed_ref[part, lanes] = sums * inverse


def copy_mass(mass_ref, mass_s):
    mass_s[...] = mass_ref[...].astype(f32).astype(bf16)


def first_kernel(row0, parts, *refs):
    seen = refs[:parts]
    coefficients, mass_ref = refs[parts : parts + 5], refs[parts + 5]
    growth_ref, flux_ref, consumed_ref = refs[parts + 6 : parts + 9]
    mass_s, *work = refs[parts + 9 :]
    copy_mass(mass_ref, mass_s)
    growth_ref[...] = jnp.zeros_like(growth_ref)
    flux_ref[...] = jnp.zeros_like(flux_ref)
    uptake_sums(row0, seen, *coefficients, mass_s, growth_ref, flux_ref, consumed_ref, *work)


def finish(flux_ref, mass_ref, secretion_ref, consumed_refs, net_refs):
    cells = flux_ref.shape[1]
    for tile in range(cells // WIDE):
        lanes = slice(tile * WIDE, (tile + 1) * WIDE)
        product = (mass_ref[:, lanes].astype(f32) * flux_ref[:, lanes]).astype(bf16)
        secreted = jnp.dot(secretion_ref[...], product, preferred_element_type=f32)
        consumed = [ref[:, lanes] for ref in consumed_refs]
        net = secreted - (consumed[0] if len(consumed) == 1 else jnp.concatenate(consumed, axis=0))
        start = 0
        for ref in net_refs:
            count = ref.shape[0]
            ref[:, lanes] = net[start : start + count].astype(ref.dtype)
            start += count


def second_kernel(row0, parts, owners, *refs):
    seen = refs[:parts]
    coefficients, mass_ref = refs[parts : parts + 5], refs[parts + 5]
    growth_in, flux_in, consumed_in, secretion_ref = refs[parts + 6 : parts + 10]
    growth_ref = refs[parts + 10]
    net_refs = refs[parts + 11 : parts + 11 + owners]
    flux_s, consumed_s, mass_s, *work = refs[parts + 11 + owners :]
    copy_mass(mass_ref, mass_s)
    growth_ref[...] = growth_in[...]
    flux_s[...] = flux_in[...]
    uptake_sums(row0, seen, *coefficients, mass_s, growth_ref, flux_s, consumed_s, *work)
    finish(flux_s, mass_ref, secretion_ref, (consumed_in, consumed_s), net_refs)


def only_kernel(row0, parts, owners, *refs):
    seen = refs[:parts]
    coefficients, mass_ref, secretion_ref = refs[parts : parts + 5], refs[parts + 5], refs[parts + 6]
    growth_ref = refs[parts + 7]
    net_refs = refs[parts + 8 : parts + 8 + owners]
    flux_s, consumed_s, mass_s, *work = refs[parts + 8 + owners :]
    copy_mass(mass_ref, mass_s)
    growth_ref[...] = jnp.zeros_like(growth_ref)
    flux_s[...] = jnp.zeros_like(flux_s)
    uptake_sums(row0, seen, *coefficients, mass_s, growth_ref, flux_s, consumed_s, *work)
    finish(flux_s, mass_ref, secretion_ref, (consumed_s,), net_refs)


def work_space(rows, strains, cells, resources):
    groups = strains // GROUP
    return [
        pltpu.VMEM((strains, cells), bf16),
        pltpu.VMEM((rows, cells), f32),
        pltpu.VMEM((strains, resources), f32),
        pltpu.VMEM((strains, resources), f32),
        pltpu.VMEM((GROUP, groups, GROUP, LANES), f32),
        pltpu.VMEM((GROUP, groups, GROUP, LANES), f32),
        pltpu.VMEM((rows, GROUP, cells), bf16),
    ]


def exchange(own, others, coefficients, mass, secretion):
    strains, cells = mass.shape
    held = own.shape[0]
    total = coefficients[1].shape[1]
    sums = jax.ShapeDtypeStruct((strains, cells), f32)
    nets = tuple(
        jax.ShapeDtypeStruct((held, cells), f32 if i == 0 else bf16) for i in range(total // held)
    )
    given = [pl.BlockSpec(memory_space=pltpu.SMEM)] + [whole()] * 5
    if held % GROUP:
        seen = jnp.concatenate([own] + others, axis=0)
        outs = pl.pallas_call(
            functools.partial(only_kernel, 0, 1, len(nets)),
            out_shape=(sums,) + nets,
            in_specs=[whole()] + given + [whole()],
            out_specs=(whole(),) * (1 + len(nets)),
            scratch_shapes=[pltpu.VMEM((strains, cells), f32), pltpu.VMEM((total, cells), f32)]
            + work_space(total, strains, cells, total),
            compiler_params=params(60),
            cost_estimate=estimate(total * strains * cells),
        )(seen, *coefficients, mass, secretion)
        return outs[0], outs[1:]
    growth, flux, consumed = pl.pallas_call(
        functools.partial(first_kernel, 0, 1),
        out_shape=(sums, sums, jax.ShapeDtypeStruct((held, cells), f32)),
        in_specs=[whole()] + given,
        out_specs=(whole(),) * 3,
        scratch_shapes=work_space(held, strains, cells, total),
        compiler_params=params(60),
        cost_estimate=estimate(held * strains * cells),
    )(own, *coefficients, mass)
    rest = total - held
    outs = pl.pallas_call(
        functools.partial(second_kernel, held, len(others), len(nets)),
        out_shape=(sums,) + nets,
        in_specs=[whole()] * len(others) + given + [whole()] * 4,
        out_specs=(whole(),) * (1 + len(nets)),
        scratch_shapes=[pltpu.VMEM((strains, cells), f32), pltpu.VMEM((rest, cells), f32)]
        + work_space(rest, strains, cells, total),
        compiler_params=params(60),
        cost_estimate=estimate(rest * strains * cells),
    )(*others, *coefficients, mass, growth, flux, consumed, secretion)
    return outs[0], outs[1:]


def laplace(field, low, high, planes, plane):
    cell = lax.broadcasted_iota(jnp.int32, (field[0].shape[0], plane), 1)
    z = lax.rem(cell, NZ)
    out = []
    for x in range(planes):
        v = field[x]
        beside = (low if x == 0 else field[x - 1]) + (high if x == planes - 1 else field[x + 1])
        beside += jnp.where(z == 0, v, pltpu.roll(v, 1, 1))
        beside += jnp.where(z == NZ - 1, v, pltpu.roll(v, plane - 1, 1))
        beside += jnp.where(cell < NZ, v, pltpu.roll(v, NZ, 1))
        beside += jnp.where(cell >= plane - NZ, v, pltpu.roll(v, plane - NZ, 1))
        out.append(beside - 6.0 * v)
    return out


def planes_of(ref, rows, planes, plane):
    return [ref[rows, x * plane : (x + 1) * plane].astype(f32) for x in range(planes)]


def step_kernel(planes, plane, mass_ref, low_ref, high_ref, sum_ref, maintenance_ref, motility_ref,
                growth_ref, new_ref):
    def per_group(group, _):
        rows = pl.ds(pl.multiple_of(group * GROUP, GROUP), GROUP)
        mass = planes_of(mass_ref, rows, planes, plane)
        spread = laplace(mass, low_ref[rows, :].astype(f32), high_ref[rows, :].astype(f32), planes, plane)
        maintenance = maintenance_ref[rows, :1]
        motility = motility_ref[rows, :1]
        for x in range(planes):
            lanes = slice(x * plane, (x + 1) * plane)
            growth = sum_ref[rows, lanes] - maintenance
            growth_ref[rows, lanes] = growth
            new_ref[rows, lanes] = mass[x] + time_step * (mass[x] * growth + motility * spread[x])
        return 0

    lax.fori_loop(0, mass_ref.shape[0] // GROUP, per_group, 0)


def resource_kernel(planes, plane, field_ref, low_ref, high_ref, net_ref, diffusivity_ref, supply_ref,
                    new_ref):
    rows = slice(0, field_ref.shape[0])
    field = planes_of(field_ref, rows, planes, plane)
    spread = laplace(field, low_ref[...].astype(f32), high_ref[...].astype(f32), planes, plane)
    for x in range(planes):
        lanes = slice(x * plane, (x + 1) * plane)
        change = diffusivity_ref[:, :1] * spread[x] + net_ref[:, lanes] + supply_ref[:, :1]
        new_ref[:, lanes] = field[x] + time_step * change


def column(values):
    return jnp.broadcast_to(values[:, None], (values.shape[0], LANES))


def halo(block, axis):
    count = lax.axis_size(axis)
    forward = [(i, (i + 1) % count) for i in range(count)]
    backward = [(target, source) for source, target in forward]
    low = lax.ppermute(block[:, -1, :], axis, forward)
    high = lax.ppermute(block[:, 0, :], axis, backward)
    return low, high


def shifted(value, axis, shift):
    count = lax.axis_size(axis)
    return lax.ppermute(value, axis, [(i, (i + shift) % count) for i in range(count)])


def per_device(
    biomass,
    resources,
    capacity,
    affinity,
    secretion,
    energy_yield,
    maintenance,
    motility,
    diffusivity,
    supply,
):
    strains, slab_rows, plane = biomass.shape
    cells = slab_rows * plane
    held = resources.shape[0]
    count = lax.axis_size("species")
    total = held * count
    field = resources.reshape(held, cells)
    own = field.astype(bf16)
    others = [shifted(own, "species", -j) for j in range(1, count)]
    mass = biomass.reshape(strains, cells)
    first = lax.axis_index("species") * held
    turned = lax.dynamic_slice_in_dim(jnp.concatenate([energy_yield, energy_yield]), first, total)
    inverse = column(1.0 / turned)
    secretion = lax.dynamic_slice_in_dim(jnp.concatenate([secretion, secretion]), first, total, 0)
    coefficients = (first[None].astype(jnp.int32), capacity, affinity, energy_yield[None, :], inverse)
    edges = jnp.concatenate([biomass, resources.astype(bf16)], axis=0)
    low, high = halo(edges, "space")
    low, high, secretion = lax.optimization_barrier((low, high, secretion))
    gained, nets = exchange(own, others, coefficients, mass, secretion)
    arrived = [shifted(nets[j], "species", j) for j in range(1, count)]
    sums = jax.ShapeDtypeStruct((strains, cells), f32)
    growth, new_biomass = pl.pallas_call(
        functools.partial(step_kernel, slab_rows, plane),
        out_shape=(sums, sums),
        in_specs=[whole()] * 6,
        out_specs=(whole(),) * 2,
        compiler_params=params(60),
        cost_estimate=estimate(strains * cells * 8),
    )(mass, low[:strains], high[:strains], gained, column(maintenance), column(motility))
    partial = pl.pallas_call(
        functools.partial(resource_kernel, slab_rows, plane),
        out_shape=jax.ShapeDtypeStruct((held, cells), f32),
        in_specs=[whole()] * 6,
        out_specs=whole(),
        compiler_params=params(60),
        cost_estimate=estimate(held * cells * 8),
    )(field, low[strains:], high[strains:], nets[0], column(diffusivity), column(supply))
    shape = (strains, slab_rows, plane)
    growth, new_biomass = growth.reshape(shape), new_biomass.reshape(shape)
    arrived, partial, growth, new_biomass = lax.optimization_barrier((arrived, partial, growth, new_biomass))
    received = arrived[0].astype(f32)
    for part in arrived[1:]:
        received = received + part.astype(f32)
    new_resources = partial + time_step * received
    return growth, new_biomass, new_resources.reshape(resources.shape)


def solution(mesh):
    return jax.shard_map(
        per_device,
        mesh=mesh,
        in_specs=(
            P("species", "space", None),
            P("species", "space", None),
            P("species", None),
            P("species", None),
            P(None, "species"),
            P(),
            P("species"),
            P("species"),
            P("species"),
            P("species"),
        ),
        out_specs=(
            P("species", "space", None),
            P("species", "space", None),
            P("species", "space", None),
        ),
        check_vma=False,
    )
```

```python
import functools

import jax
import jax.numpy as jnp
from jax import lax
from jax.experimental import pallas as pl
from jax.experimental.pallas import tpu as pltpu
from jax.sharding import PartitionSpec as P

NY = 16
NZ = 64

time_step = 0.25

bf16 = jnp.bfloat16
f32 = jnp.float32
LANES = 128
GROUP = 16
WIDE = 256


def whole():
    return pl.BlockSpec(memory_space=pltpu.VMEM)


def params(limit):
    return pltpu.CompilerParams(vmem_limit_bytes=limit << 20)


def estimate(elements):
    return pl.CostEstimate(flops=40 * elements, bytes_accessed=1 << 20, transcendentals=elements)


def uptake_sums(row0, seen_refs, first_ref, capacity_ref, affinity_ref, yield_ref, inverse_ref, mass_s,
                growth_ref, flux_ref, consumed_ref, y_s, slopes_s, levels_s, slope_s, level_s, eaten_s):
    rows, cells = y_s.shape
    strains, resources = capacity_ref.shape
    groups = strains // GROUP
    blocks = rows // GROUP
    start = 0
    for ref in seen_refs:
        count = ref.shape[0]
        y_s[start : start + count, :] = 1.0 / ref[...].astype(f32)
        start += count
    turn = lax.rem(2 * resources - first_ref[0] - row0, resources)
    level = 1.0 / (capacity_ref[...] * yield_ref[...])
    slopes_s[...] = pltpu.roll(affinity_ref[...] * level, turn, 1)
    levels_s[...] = pltpu.roll(level, turn, 1)

    def per_block(block, _):
        r0 = pl.multiple_of(block * GROUP, GROUP)
        turn = lax.rem(resources - r0, resources)
        members = [pl.ds(g * GROUP, GROUP) for g in range(groups)]
        slopes = [pltpu.roll(slopes_s[m, :], turn, 1) for m in members]
        levels = [pltpu.roll(levels_s[m, :], turn, 1) for m in members]
        for r in range(GROUP):
            for g in range(groups):
                slope_s[r, g] = jnp.broadcast_to(slopes[g][:, r : r + 1], (GROUP, LANES))
                level_s[r, g] = jnp.broadcast_to(levels[g][:, r : r + 1], (GROUP, LANES))

        def per_tile(tile, _):
            lanes = pl.ds(pl.multiple_of(tile * LANES, LANES), LANES)
            y_rows = y_s[pl.ds(r0, GROUP), lanes]
            inverse = inverse_ref[pl.ds(row0 + r0, GROUP), :]
            growth = [growth_ref[g * GROUP : (g + 1) * GROUP, lanes] for g in range(groups)]
            flux = [None] * groups
            for r in range(GROUP):
                y = jnp.broadcast_to(y_rows[r : r + 1], (GROUP, LANES))
                scale = jnp.broadcast_to(inverse[r : r + 1], (GROUP, LANES)).astype(bf16)
                eaten = None
                for g in range(groups):
                    gain = pl.reciprocal(slope_s[r, g] * y + level_s[r, g], approx=True)
                    growth[g] = growth[g] + gain
                    short = gain.astype(bf16)
                    taken = short * scale
                    flux[g] = taken if r == 0 else flux[g] + taken
                    part = short * mass_s[g * GROUP : (g + 1) * GROUP, lanes]
                    eaten = part if g == 0 else eaten + part
                eaten_s[r0 + r, :, lanes] = eaten
            for g in range(groups):
                strains = slice(g * GROUP, (g + 1) * GROUP)
                growth_ref[strains, lanes] = growth[g]
                flux_ref[strains, lanes] += flux[g].astype(f32)
            return 0

        lax.fori_loop(0, cells // LANES, per_tile, 0)
        return 0

    lax.fori_loop(0, blocks, per_block, 0)

    shape = (GROUP, GROUP * GROUP)
    ones = lax.broadcasted_iota(jnp.int32, shape, 1) // GROUP
    ones = (ones == lax.broadcasted_iota(jnp.int32, shape, 0)).astype(f32).astype(bf16)
    for block in range(blocks):
        part = slice(block * GROUP, (block + 1) * GROUP)
        inverse = inverse_ref[row0 + block * GROUP : row0 + (block + 1) * GROUP, :1]
        for tile in range(cells // WIDE):
            lanes = slice(tile * WIDE, (tile + 1) * WIDE)
            sums = jnp.dot(
                ones, eaten_s[part, :, lanes].reshape(GROUP * GROUP, WIDE), preferred_element_type=f32
            )
            consumed_ref[part, lanes] = sums * inverse


def copy_mass(mass_ref, mass_s):
    mass_s[...] = mass_ref[...].astype(f32).astype(bf16)


def first_kernel(row0, parts, *refs):
    seen = refs[:parts]
    coefficients, mass_ref = refs[parts : parts + 5], refs[parts + 5]
    growth_ref, flux_ref, consumed_ref = refs[parts + 6 : parts + 9]
    mass_s, *work = refs[parts + 9 :]
    copy_mass(mass_ref, mass_s)
    growth_ref[...] = jnp.zeros_like(growth_ref)
    flux_ref[...] = jnp.zeros_like(flux_ref)
    uptake_sums(row0, seen, *coefficients, mass_s, growth_ref, flux_ref, consumed_ref, *work)


def finish(flux_ref, mass_ref, secretion_ref, consumed_refs, net_refs):
    cells = flux_ref.shape[1]
    base = None
    for tile in range(cells // WIDE):
        lanes = slice(tile * WIDE, (tile + 1) * WIDE)
        product = (mass_ref[:, lanes].astype(f32) * flux_ref[:, lanes]).astype(bf16)
        secreted = jnp.dot(secretion_ref[...], product, preferred_element_type=f32)
        consumed = [ref[:, lanes] for ref in consumed_refs]
        net = secreted - (consumed[0] if len(consumed) == 1 else jnp.concatenate(consumed, axis=0))
        if base is None:
            base = jnp.mean(net, axis=1, keepdims=True).astype(bf16).astype(f32)
            base = jnp.broadcast_to(base, (net.shape[0], LANES))
        start = 0
        for ref in net_refs:
            rows = slice(start, start + ref.shape[0])
            start += ref.shape[0]
            if ref.dtype == f32:
                ref[:, lanes] = net[rows]
                continue
            ref[:, lanes] = (net[rows] - base[rows, :1]).astype(bf16)
            if tile == 0:
                ref[:, cells : cells + LANES] = base[rows].astype(bf16)


def second_kernel(row0, parts, owners, *refs):
    seen = refs[:parts]
    coefficients, mass_ref = refs[parts : parts + 5], refs[parts + 5]
    growth_in, flux_in, consumed_in, secretion_ref = refs[parts + 6 : parts + 10]
    growth_ref = refs[parts + 10]
    net_refs = refs[parts + 11 : parts + 11 + owners]
    flux_s, consumed_s, mass_s, *work = refs[parts + 11 + owners :]
    copy_mass(mass_ref, mass_s)
    growth_ref[...] = growth_in[...]
    flux_s[...] = flux_in[...]
    uptake_sums(row0, seen, *coefficients, mass_s, growth_ref, flux_s, consumed_s, *work)
    finish(flux_s, mass_ref, secretion_ref, (consumed_in, consumed_s), net_refs)


def only_kernel(row0, parts, owners, *refs):
    seen = refs[:parts]
    coefficients, mass_ref, secretion_ref = refs[parts : parts + 5], refs[parts + 5], refs[parts + 6]
    growth_ref = refs[parts + 7]
    net_refs = refs[parts + 8 : parts + 8 + owners]
    flux_s, consumed_s, mass_s, *work = refs[parts + 8 + owners :]
    copy_mass(mass_ref, mass_s)
    growth_ref[...] = jnp.zeros_like(growth_ref)
    flux_s[...] = jnp.zeros_like(flux_s)
    uptake_sums(row0, seen, *coefficients, mass_s, growth_ref, flux_s, consumed_s, *work)
    finish(flux_s, mass_ref, secretion_ref, (consumed_s,), net_refs)


def work_space(rows, strains, cells, resources):
    groups = strains // GROUP
    return [
        pltpu.VMEM((strains, cells), bf16),
        pltpu.VMEM((rows, cells), f32),
        pltpu.VMEM((strains, resources), f32),
        pltpu.VMEM((strains, resources), f32),
        pltpu.VMEM((GROUP, groups, GROUP, LANES), f32),
        pltpu.VMEM((GROUP, groups, GROUP, LANES), f32),
        pltpu.VMEM((rows, GROUP, cells), bf16),
    ]


def exchange(own, others, coefficients, mass, secretion, edges):
    strains, cells = mass.shape
    held = own.shape[0]
    total = coefficients[1].shape[1]
    sums = jax.ShapeDtypeStruct((strains, cells), f32)
    nets = tuple(
        jax.ShapeDtypeStruct((held, cells) if i == 0 else (held, cells + LANES), f32 if i == 0 else bf16)
        for i in range(total // held)
    )
    given = [pl.BlockSpec(memory_space=pltpu.SMEM)] + [whole()] * 5
    if held % GROUP:
        seen = jnp.concatenate([own] + others, axis=0)
        outs = pl.pallas_call(
            functools.partial(only_kernel, 0, 1, len(nets)),
            out_shape=(sums,) + nets,
            in_specs=[whole()] + given + [whole()],
            out_specs=(whole(),) * (1 + len(nets)),
            scratch_shapes=[pltpu.VMEM((strains, cells), f32), pltpu.VMEM((total, cells), f32)]
            + work_space(total, strains, cells, total),
            compiler_params=params(60),
            cost_estimate=estimate(total * strains * cells),
        )(seen, *coefficients, mass, secretion)
        return *halo(edges, "space"), outs[0], outs[1:]
    growth, flux, consumed = pl.pallas_call(
        functools.partial(first_kernel, 0, 1),
        out_shape=(sums, sums, jax.ShapeDtypeStruct((held, cells), f32)),
        in_specs=[whole()] + given,
        out_specs=(whole(),) * 3,
        scratch_shapes=work_space(held, strains, cells, total),
        compiler_params=params(60),
        cost_estimate=estimate(held * strains * cells),
    )(own, *coefficients, mass)
    edges, consumed = lax.optimization_barrier((edges, consumed))
    low, high = halo(edges, "space")
    rest = total - held
    outs = pl.pallas_call(
        functools.partial(second_kernel, held, len(others), len(nets)),
        out_shape=(sums,) + nets,
        in_specs=[whole()] * len(others) + given + [whole()] * 4,
        out_specs=(whole(),) * (1 + len(nets)),
        scratch_shapes=[pltpu.VMEM((strains, cells), f32), pltpu.VMEM((rest, cells), f32)]
        + work_space(rest, strains, cells, total),
        compiler_params=params(60),
        cost_estimate=estimate(rest * strains * cells),
    )(*others, *coefficients, mass, growth, flux, consumed, secretion)
    return low, high, outs[0], outs[1:]


def laplace(field, low, high, planes, plane):
    cell = lax.broadcasted_iota(jnp.int32, (field[0].shape[0], plane), 1)
    z = lax.rem(cell, NZ)
    out = []
    for x in range(planes):
        v = field[x]
        beside = (low if x == 0 else field[x - 1]) + (high if x == planes - 1 else field[x + 1])
        beside += jnp.where(z == 0, v, pltpu.roll(v, 1, 1))
        beside += jnp.where(z == NZ - 1, v, pltpu.roll(v, plane - 1, 1))
        beside += jnp.where(cell < NZ, v, pltpu.roll(v, NZ, 1))
        beside += jnp.where(cell >= plane - NZ, v, pltpu.roll(v, plane - NZ, 1))
        out.append(beside - 6.0 * v)
    return out


def planes_of(ref, rows, planes, plane):
    return [ref[rows, x * plane : (x + 1) * plane].astype(f32) for x in range(planes)]


def column(row):
    size = row.shape[1]
    shape = (size, size)
    own = lax.broadcasted_iota(jnp.int32, shape, 0) == lax.broadcasted_iota(jnp.int32, shape, 1)
    return jnp.sum(jnp.where(own, jnp.broadcast_to(row, shape), 0.0), axis=1, keepdims=True)


def step_kernel(planes, plane, mass_ref, field_ref, low_ref, high_ref, sum_ref, net_ref, maintenance_ref,
                motility_ref, diffusivity_ref, supply_ref, growth_ref, new_ref, partial_ref, traits_s):
    strains = mass_ref.shape[0]
    held = field_ref.shape[0]
    traits_s[:, 0:1] = column(maintenance_ref[...])
    traits_s[:, 1:2] = column(motility_ref[...])

    def per_group(group, _):
        rows = pl.ds(pl.multiple_of(group * GROUP, GROUP), GROUP)
        mass = planes_of(mass_ref, rows, planes, plane)
        spread = laplace(mass, low_ref[rows, :].astype(f32), high_ref[rows, :].astype(f32), planes, plane)
        maintenance = traits_s[rows, 0:1]
        motility = traits_s[rows, 1:2]
        for x in range(planes):
            growth = sum_ref[rows, x * plane : (x + 1) * plane] - maintenance
            growth_ref[rows, x, :] = growth
            new_ref[rows, x, :] = mass[x] + time_step * (mass[x] * growth + motility * spread[x])
        return 0

    lax.fori_loop(0, strains // GROUP, per_group, 0)
    field = planes_of(field_ref, slice(0, held), planes, plane)
    beyond = slice(strains, strains + held)
    spread = laplace(field, low_ref[beyond, :].astype(f32), high_ref[beyond, :].astype(f32), planes, plane)
    diffusivity = column(diffusivity_ref[...])
    supply = column(supply_ref[...])
    for x in range(planes):
        lanes = slice(x * plane, (x + 1) * plane)
        change = diffusivity * spread[x] + net_ref[:, lanes] + supply
        partial_ref[:, lanes] = field[x] + time_step * change


def close_kernel(planes, plane, partial_ref, *refs):
    *arrived, new_ref = refs
    cells = planes * plane
    base = sum(ref[:, cells : cells + LANES].astype(f32) for ref in arrived)[:, :1]
    for x in range(planes):
        lanes = slice(x * plane, (x + 1) * plane)
        net = sum(ref[:, lanes].astype(f32) for ref in arrived) + base
        new_ref[:, x, :] = partial_ref[:, lanes] + time_step * net


def halo(block, axis):
    count = lax.axis_size(axis)
    forward = [(i, (i + 1) % count) for i in range(count)]
    backward = [(target, source) for source, target in forward]
    low = lax.ppermute(block[:, -1, :], axis, forward)
    high = lax.ppermute(block[:, 0, :], axis, backward)
    return low, high


def shifted(value, axis, shift):
    count = lax.axis_size(axis)
    return lax.ppermute(value, axis, [(i, (i + shift) % count) for i in range(count)])


def per_device(
    biomass,
    resources,
    capacity,
    affinity,
    secretion,
    energy_yield,
    maintenance,
    motility,
    diffusivity,
    supply,
):
    strains, slab_rows, plane = biomass.shape
    cells = slab_rows * plane
    held = resources.shape[0]
    count = lax.axis_size("species")
    total = held * count
    field = resources.reshape(held, cells)
    own = field.astype(bf16)
    others = [shifted(own, "species", -j) for j in range(1, count)]
    mass = biomass.reshape(strains, cells)
    first = lax.axis_index("species") * held
    turned = lax.dynamic_slice_in_dim(jnp.concatenate([energy_yield, energy_yield]), first, total)
    inverse = jnp.broadcast_to((1.0 / turned)[:, None], (total, LANES))
    secretion = lax.dynamic_slice_in_dim(jnp.concatenate([secretion, secretion]), first, total, 0)
    coefficients = (first[None].astype(jnp.int32), capacity, affinity, energy_yield[None, :], inverse)
    edges = jnp.concatenate([biomass, resources.astype(bf16)], axis=0)
    low, high, gained, nets = exchange(own, others, coefficients, mass, secretion, edges)
    arrived = [shifted(nets[j], "species", j) for j in range(1, count)]
    sums = jax.ShapeDtypeStruct(biomass.shape, f32)
    growth, new_biomass, partial = pl.pallas_call(
        functools.partial(step_kernel, slab_rows, plane),
        out_shape=(sums, sums, jax.ShapeDtypeStruct((held, cells), f32)),
        in_specs=[whole()] * 10,
        out_specs=(whole(),) * 3,
        scratch_shapes=[pltpu.VMEM((strains, LANES), f32)],
        compiler_params=params(60),
        cost_estimate=estimate(strains * cells * 8),
    )(mass, field, low, high, gained, nets[0], maintenance[None, :], motility[None, :],
      diffusivity[None, :], supply[None, :])
    arrived, partial = lax.optimization_barrier((arrived, partial))
    new_resources = pl.pallas_call(
        functools.partial(close_kernel, slab_rows, plane),
        out_shape=jax.ShapeDtypeStruct(resources.shape, f32),
        in_specs=[whole()] * count,
        out_specs=whole(),
        compiler_params=params(60),
        cost_estimate=estimate(held * cells),
    )(partial, *arrived)
    return growth, new_biomass, new_resources


def solution(mesh):
    return jax.shard_map(
        per_device,
        mesh=mesh,
        in_specs=(
            P("species", "space", None),
            P("species", "space", None),
            P("species", None),
            P("species", None),
            P(None, "species"),
            P(),
            P("species"),
            P("species"),
            P("species"),
            P("species"),
        ),
        out_specs=(
            P("species", "space", None),
            P("species", "space", None),
            P("species", "space", None),
        ),
        check_vma=False,
    )
```

```python
import functools

import jax
import jax.numpy as jnp
from jax import lax
from jax.experimental import pallas as pl
from jax.experimental.pallas import tpu as pltpu
from jax.sharding import PartitionSpec as P

NY = 16
NZ = 64

time_step = 0.25

bf16 = jnp.bfloat16
f32 = jnp.float32
LANES = 128
GROUP = 16
WIDE = 256


def whole():
    return pl.BlockSpec(memory_space=pltpu.VMEM)


def params(limit):
    return pltpu.CompilerParams(vmem_limit_bytes=limit << 20)


def estimate(elements):
    return pl.CostEstimate(flops=40 * elements, bytes_accessed=1 << 20, transcendentals=elements)


def column(row):
    size = row.shape[1]
    shape = (size, size)
    own = lax.broadcasted_iota(jnp.int32, shape, 0) == lax.broadcasted_iota(jnp.int32, shape, 1)
    return jnp.sum(jnp.where(own, jnp.broadcast_to(row, shape), 0.0), axis=1, keepdims=True)


def uptake_sums(row0, seen_refs, first_ref, capacity_ref, affinity_ref, yield_ref, mass_s, growth_ref,
                flux_ref, consumed_ref, y_s, slopes_s, levels_s, inverse_s, spread_s, eaten_s):
    rows, cells = y_s.shape
    strains, resources = capacity_ref.shape
    groups = strains // GROUP
    blocks = rows // GROUP
    tiles = cells // LANES
    start = 0
    eaten_s[0:GROUP] = jnp.zeros_like(eaten_s[0:GROUP])
    for ref in seen_refs:
        count = ref.shape[0]
        y_s[start : start + count, :] = 1.0 / ref[...].astype(f32)
        start += count
    turn = lax.rem(2 * resources - first_ref[0] - row0, resources)
    level = 1.0 / (capacity_ref[...] * yield_ref[...])
    slopes_s[...] = pltpu.roll(affinity_ref[...] * level, turn, 1)
    levels_s[...] = pltpu.roll(level, turn, 1)
    inverse_s[...] = jnp.broadcast_to(1.0 / column(pltpu.roll(yield_ref[...], turn, 1))[:rows], inverse_s.shape)

    shape = (GROUP, GROUP * GROUP)
    ones = lax.broadcasted_iota(jnp.int32, shape, 1) // GROUP
    ones = (ones == lax.broadcasted_iota(jnp.int32, shape, 0)).astype(f32).astype(bf16)

    def sum_block(block):
        part = pl.ds(pl.multiple_of(block * GROUP, GROUP), GROUP)
        inverse = inverse_s[part, :1]
        for tile in range(cells // WIDE):
            lanes = slice(tile * WIDE, (tile + 1) * WIDE)
            eaten = eaten_s[part, :, lanes].reshape(GROUP * GROUP, WIDE)
            consumed_ref[part, lanes] = jnp.dot(ones, eaten, preferred_element_type=f32) * inverse

    def per_block(block, _):
        r0 = pl.multiple_of(block * GROUP, GROUP)
        for r in range(GROUP):
            chosen = jnp.full((GROUP, LANES), r0 + r, jnp.int32)
            for g in range(groups):
                members = slice(g * GROUP, (g + 1) * GROUP)
                spread_s[0, r, g] = jnp.take_along_axis(slopes_s[members, :], chosen, axis=1)
                spread_s[1, r, g] = jnp.take_along_axis(levels_s[members, :], chosen, axis=1)

        sum_block(jnp.maximum(block - 1, 0))

        def per_tile(tile, _):
            lanes = pl.ds(pl.multiple_of(tile * LANES, LANES), LANES)
            y_rows = y_s[pl.ds(r0, GROUP), lanes]
            inverse = inverse_s[pl.ds(r0, GROUP), :]
            growth = [growth_ref[g * GROUP : (g + 1) * GROUP, lanes] for g in range(groups)]
            flux = [None] * groups
            for r in range(GROUP):
                y = jnp.broadcast_to(y_rows[r : r + 1], (GROUP, LANES))
                scale = jnp.broadcast_to(inverse[r : r + 1], (GROUP, LANES)).astype(bf16)
                eaten = None
                for g in range(groups):
                    gain = pl.reciprocal(spread_s[0, r, g] * y + spread_s[1, r, g], approx=True)
                    growth[g] = growth[g] + gain
                    short = gain.astype(bf16)
                    taken = short * scale
                    flux[g] = taken if r == 0 else flux[g] + taken
                    part = short * mass_s[g * GROUP : (g + 1) * GROUP, lanes]
                    eaten = part if g == 0 else eaten + part
                eaten_s[r0 + r, :, lanes] = eaten
            for g in range(groups):
                strains = slice(g * GROUP, (g + 1) * GROUP)
                growth_ref[strains, lanes] = growth[g]
                flux_ref[strains, lanes] += flux[g].astype(f32)
            return 0

        lax.fori_loop(0, tiles, per_tile, 0, unroll=4)
        return 0

    lax.fori_loop(0, blocks, per_block, 0)
    sum_block(blocks - 1)


def copy_mass(mass_ref, mass_s):
    mass_s[...] = mass_ref[...].astype(f32).astype(bf16)


def first_kernel(row0, parts, *refs):
    seen = refs[:parts]
    coefficients, mass_ref = refs[parts : parts + 4], refs[parts + 4]
    growth_ref, flux_ref, consumed_ref = refs[parts + 5 : parts + 8]
    mass_s, *work = refs[parts + 8 :]
    copy_mass(mass_ref, mass_s)
    growth_ref[...] = jnp.zeros_like(growth_ref)
    flux_ref[...] = jnp.zeros_like(flux_ref)
    uptake_sums(row0, seen, *coefficients, mass_s, growth_ref, flux_ref, consumed_ref, *work)


def finish(first_ref, flux_ref, mass_ref, secretion_ref, consumed_refs, net_refs):
    cells = flux_ref.shape[1]
    resources = secretion_ref.shape[0]
    turn = lax.rem(resources - first_ref[0], resources)
    secretion = pltpu.roll(secretion_ref[...].astype(f32), turn, 0).astype(bf16)
    base = None
    for tile in range(cells // WIDE):
        lanes = slice(tile * WIDE, (tile + 1) * WIDE)
        product = (mass_ref[:, lanes].astype(f32) * flux_ref[:, lanes]).astype(bf16)
        secreted = jnp.dot(secretion, product, preferred_element_type=f32)
        consumed = [ref[:, lanes] for ref in consumed_refs]
        net = secreted - (consumed[0] if len(consumed) == 1 else jnp.concatenate(consumed, axis=0))
        if base is None:
            base = jnp.mean(net, axis=1, keepdims=True).astype(bf16).astype(f32)
            base = jnp.broadcast_to(base, (net.shape[0], LANES))
        start = 0
        for ref in net_refs:
            rows = slice(start, start + ref.shape[0])
            start += ref.shape[0]
            if ref.dtype == f32:
                ref[:, lanes] = net[rows]
                continue
            ref[:, lanes] = (net[rows] - base[rows, :1]).astype(bf16)
            if tile == 0:
                ref[:, cells : cells + LANES] = base[rows].astype(bf16)


def second_kernel(row0, parts, owners, *refs):
    seen = refs[:parts]
    coefficients, mass_ref = refs[parts : parts + 4], refs[parts + 4]
    growth_in, flux_in, consumed_in, secretion_ref = refs[parts + 5 : parts + 9]
    growth_ref = refs[parts + 9]
    net_refs = refs[parts + 10 : parts + 10 + owners]
    flux_s, consumed_s, mass_s, *work = refs[parts + 10 + owners :]
    copy_mass(mass_ref, mass_s)
    growth_ref[...] = growth_in[...]
    flux_s[...] = flux_in[...]
    uptake_sums(row0, seen, *coefficients, mass_s, growth_ref, flux_s, consumed_s, *work)
    finish(coefficients[0], flux_s, mass_ref, secretion_ref, (consumed_in, consumed_s), net_refs)


def only_kernel(row0, parts, owners, *refs):
    seen = refs[:parts]
    coefficients, mass_ref, secretion_ref = refs[parts : parts + 4], refs[parts + 4], refs[parts + 5]
    growth_ref = refs[parts + 6]
    net_refs = refs[parts + 7 : parts + 7 + owners]
    flux_s, consumed_s, mass_s, *work = refs[parts + 7 + owners :]
    copy_mass(mass_ref, mass_s)
    growth_ref[...] = jnp.zeros_like(growth_ref)
    flux_s[...] = jnp.zeros_like(flux_s)
    uptake_sums(row0, seen, *coefficients, mass_s, growth_ref, flux_s, consumed_s, *work)
    finish(coefficients[0], flux_s, mass_ref, secretion_ref, (consumed_s,), net_refs)


def work_space(rows, strains, cells, resources):
    groups = strains // GROUP
    return [
        pltpu.VMEM((strains, cells), bf16),
        pltpu.VMEM((rows, cells), f32),
        pltpu.VMEM((strains, resources), f32),
        pltpu.VMEM((strains, resources), f32),
        pltpu.VMEM((rows, LANES), f32),
        pltpu.VMEM((2, GROUP, groups, GROUP, LANES), f32),
        pltpu.VMEM((rows, GROUP, cells), bf16),
    ]


def exchange(own, others, coefficients, mass, secretion, edges):
    strains, cells = mass.shape
    held = own.shape[0]
    total = coefficients[1].shape[1]
    sums = jax.ShapeDtypeStruct((strains, cells), f32)
    nets = tuple(
        jax.ShapeDtypeStruct((held, cells) if i == 0 else (held, cells + LANES), f32 if i == 0 else bf16)
        for i in range(total // held)
    )
    given = [pl.BlockSpec(memory_space=pltpu.SMEM)] + [whole()] * 4
    if held % GROUP:
        seen = jnp.concatenate([own] + others, axis=0)
        outs = pl.pallas_call(
            functools.partial(only_kernel, 0, 1, len(nets)),
            out_shape=(sums,) + nets,
            in_specs=[whole()] + given + [whole()],
            out_specs=(whole(),) * (1 + len(nets)),
            scratch_shapes=[pltpu.VMEM((strains, cells), f32), pltpu.VMEM((total, cells), f32)]
            + work_space(total, strains, cells, total),
            compiler_params=params(60),
            cost_estimate=estimate(total * strains * cells),
        )(seen, *coefficients, mass, secretion)
        return *halo(edges, "space"), outs[0], outs[1:]
    growth, flux, consumed = pl.pallas_call(
        functools.partial(first_kernel, 0, 1),
        out_shape=(sums, sums, jax.ShapeDtypeStruct((held, cells), f32)),
        in_specs=[whole()] + given,
        out_specs=(whole(),) * 3,
        scratch_shapes=work_space(held, strains, cells, total),
        compiler_params=params(60),
        cost_estimate=estimate(held * strains * cells),
    )(own, *coefficients, mass)
    edges, consumed = lax.optimization_barrier((edges, consumed))
    low, high = halo(edges, "space")
    rest = total - held
    outs = pl.pallas_call(
        functools.partial(second_kernel, held, len(others), len(nets)),
        out_shape=(sums,) + nets,
        in_specs=[whole()] * len(others) + given + [whole()] * 4,
        out_specs=(whole(),) * (1 + len(nets)),
        scratch_shapes=[pltpu.VMEM((strains, cells), f32), pltpu.VMEM((rest, cells), f32)]
        + work_space(rest, strains, cells, total),
        compiler_params=params(60),
        cost_estimate=estimate(rest * strains * cells),
    )(*others, *coefficients, mass, growth, flux, consumed, secretion)
    return low, high, outs[0], outs[1:]


def laplace(field, low, high, planes, plane):
    cell = lax.broadcasted_iota(jnp.int32, (field[0].shape[0], plane), 1)
    z = lax.rem(cell, NZ)
    out = []
    for x in range(planes):
        v = field[x]
        beside = (low if x == 0 else field[x - 1]) + (high if x == planes - 1 else field[x + 1])
        beside += jnp.where(z == 0, v, pltpu.roll(v, 1, 1))
        beside += jnp.where(z == NZ - 1, v, pltpu.roll(v, plane - 1, 1))
        beside += jnp.where(cell < NZ, v, pltpu.roll(v, NZ, 1))
        beside += jnp.where(cell >= plane - NZ, v, pltpu.roll(v, plane - NZ, 1))
        out.append(beside - 6.0 * v)
    return out


def planes_of(ref, rows, planes, plane):
    return [ref[rows, x * plane : (x + 1) * plane].astype(f32) for x in range(planes)]


def step_kernel(planes, plane, mass_ref, field_ref, low_ref, high_ref, sum_ref, net_ref, maintenance_ref,
                motility_ref, diffusivity_ref, supply_ref, growth_ref, new_ref, partial_ref, traits_s):
    strains = mass_ref.shape[0]
    held = field_ref.shape[0]
    traits_s[:, 0:1] = column(maintenance_ref[...])
    traits_s[:, 1:2] = column(motility_ref[...])

    def per_group(group, _):
        rows = pl.ds(pl.multiple_of(group * GROUP, GROUP), GROUP)
        mass = planes_of(mass_ref, rows, planes, plane)
        spread = laplace(mass, low_ref[rows, :].astype(f32), high_ref[rows, :].astype(f32), planes, plane)
        maintenance = traits_s[rows, 0:1]
        motility = traits_s[rows, 1:2]
        for x in range(planes):
            growth = sum_ref[rows, x * plane : (x + 1) * plane] - maintenance
            growth_ref[rows, x, :] = growth
            new_ref[rows, x, :] = mass[x] + time_step * (mass[x] * growth + motility * spread[x])
        return 0

    lax.fori_loop(0, strains // GROUP, per_group, 0)
    field = planes_of(field_ref, slice(0, held), planes, plane)
    beyond = slice(strains, strains + held)
    spread = laplace(field, low_ref[beyond, :].astype(f32), high_ref[beyond, :].astype(f32), planes, plane)
    diffusivity = column(diffusivity_ref[...])
    supply = column(supply_ref[...])
    for x in range(planes):
        lanes = slice(x * plane, (x + 1) * plane)
        change = diffusivity * spread[x] + net_ref[:, lanes] + supply
        partial_ref[:, lanes] = field[x] + time_step * change


def halo(block, axis):
    count = lax.axis_size(axis)
    forward = [(i, (i + 1) % count) for i in range(count)]
    backward = [(target, source) for source, target in forward]
    low = lax.ppermute(block[:, -1, :], axis, forward)
    high = lax.ppermute(block[:, 0, :], axis, backward)
    return low, high


def shifted(value, axis, shift):
    count = lax.axis_size(axis)
    return lax.ppermute(value, axis, [(i, (i + shift) % count) for i in range(count)])


def per_device(
    biomass,
    resources,
    capacity,
    affinity,
    secretion,
    energy_yield,
    maintenance,
    motility,
    diffusivity,
    supply,
):
    strains, slab_rows, plane = biomass.shape
    cells = slab_rows * plane
    held = resources.shape[0]
    count = lax.axis_size("species")
    total = held * count
    field = resources.reshape(held, cells)
    own = field.astype(bf16)
    others = [shifted(own, "species", -j) for j in range(1, count)]
    mass = biomass.reshape(strains, cells)
    first = lax.axis_index("species") * held
    coefficients = (first[None].astype(jnp.int32), capacity, affinity, energy_yield[None, :])
    edges = jnp.concatenate([biomass, resources.astype(bf16)], axis=0)
    low, high, gained, nets = exchange(own, others, coefficients, mass, secretion, edges)
    arrived = [shifted(nets[j], "species", j) for j in range(1, count)]
    sums = jax.ShapeDtypeStruct(biomass.shape, f32)
    growth, new_biomass, partial = pl.pallas_call(
        functools.partial(step_kernel, slab_rows, plane),
        out_shape=(sums, sums, jax.ShapeDtypeStruct((held, cells), f32)),
        in_specs=[whole()] * 10,
        out_specs=(whole(),) * 3,
        scratch_shapes=[pltpu.VMEM((strains, LANES), f32)],
        compiler_params=params(60),
        cost_estimate=estimate(strains * cells * 8),
    )(mass, field, low, high, gained, nets[0], maintenance[None, :], motility[None, :],
      diffusivity[None, :], supply[None, :])
    arrived, partial = lax.optimization_barrier((arrived, partial))
    received = sum(part[:, :cells].astype(f32) + part[:, cells : cells + 1].astype(f32) for part in arrived)
    new_resources = (partial + time_step * received).reshape(resources.shape)
    return growth, new_biomass, new_resources


def solution(mesh):
    return jax.shard_map(
        per_device,
        mesh=mesh,
        in_specs=(
            P("species", "space", None),
            P("species", "space", None),
            P("species", None),
            P("species", None),
            P(None, "species"),
            P(),
            P("species"),
            P("species"),
            P("species"),
            P("species"),
        ),
        out_specs=(
            P("species", "space", None),
            P("species", "space", None),
            P("species", "space", None),
        ),
        check_vma=False,
    )
```

```python
import functools

import jax
import jax.numpy as jnp
from jax import lax
from jax.experimental import pallas as pl
from jax.experimental.pallas import tpu as pltpu
from jax.sharding import PartitionSpec as P

NY = 16
NZ = 64

time_step = 0.25

bf16 = jnp.bfloat16
f32 = jnp.float32
LANES = 128
GROUP = 16
WIDE = 256


def whole():
    return pl.BlockSpec(memory_space=pltpu.VMEM)


def params(limit):
    return pltpu.CompilerParams(vmem_limit_bytes=limit << 20)


def estimate(elements):
    return pl.CostEstimate(flops=40 * elements, bytes_accessed=1 << 20, transcendentals=elements)


def column(row):
    size = row.shape[1]
    shape = (size, size)
    own = lax.broadcasted_iota(jnp.int32, shape, 0) == lax.broadcasted_iota(jnp.int32, shape, 1)
    return jnp.sum(jnp.where(own, jnp.broadcast_to(row, shape), 0.0), axis=1, keepdims=True)


def uptake_sums(row0, seen_refs, first_ref, capacity_ref, affinity_ref, yield_ref, mass_s, growth_ref,
                flux_ref, consumed_ref, y_s, slopes_s, levels_s, inverse_s, spread_s, eaten_s):
    rows, cells = y_s.shape
    strains, resources = capacity_ref.shape
    groups = strains // GROUP
    blocks = rows // GROUP
    tiles = cells // LANES
    start = 0
    eaten_s[0:GROUP] = jnp.zeros_like(eaten_s[0:GROUP])
    for ref in seen_refs:
        count = ref.shape[0]
        y_s[start : start + count, :] = 1.0 / ref[...].astype(f32)
        start += count
    turn = lax.rem(2 * resources - first_ref[0] - row0, resources)
    level = 1.0 / (capacity_ref[...] * yield_ref[...])
    slopes_s[...] = pltpu.roll(affinity_ref[...] * level, turn, 1)
    levels_s[...] = pltpu.roll(level, turn, 1)
    inverse_s[...] = jnp.broadcast_to(1.0 / column(pltpu.roll(yield_ref[...], turn, 1))[:rows], inverse_s.shape)

    shape = (GROUP, GROUP * GROUP)
    ones = lax.broadcasted_iota(jnp.int32, shape, 1) // GROUP
    ones = (ones == lax.broadcasted_iota(jnp.int32, shape, 0)).astype(f32).astype(bf16)

    def sum_block(block):
        part = pl.ds(pl.multiple_of(block * GROUP, GROUP), GROUP)
        inverse = inverse_s[part, :1]
        for tile in range(cells // WIDE):
            lanes = slice(tile * WIDE, (tile + 1) * WIDE)
            eaten = eaten_s[part, :, lanes].reshape(GROUP * GROUP, WIDE)
            consumed_ref[part, lanes] = jnp.dot(ones, eaten, preferred_element_type=f32) * inverse

    def per_block(block, _):
        r0 = pl.multiple_of(block * GROUP, GROUP)
        for r in range(GROUP):
            chosen = jnp.full((GROUP, LANES), r0 + r, jnp.int32)
            for g in range(groups):
                members = slice(g * GROUP, (g + 1) * GROUP)
                spread_s[0, r, g] = jnp.take_along_axis(slopes_s[members, :], chosen, axis=1)
                spread_s[1, r, g] = jnp.take_along_axis(levels_s[members, :], chosen, axis=1)

        sum_block(jnp.maximum(block - 1, 0))

        def per_tile(tile, _):
            lanes = pl.ds(pl.multiple_of(tile * LANES, LANES), LANES)
            y_rows = y_s[pl.ds(r0, GROUP), lanes]
            inverse = inverse_s[pl.ds(r0, GROUP), :]
            growth = [growth_ref[g * GROUP : (g + 1) * GROUP, lanes] for g in range(groups)]
            flux = [None] * groups
            for r in range(GROUP):
                y = jnp.broadcast_to(y_rows[r : r + 1], (GROUP, LANES))
                scale = jnp.broadcast_to(inverse[r : r + 1], (GROUP, LANES)).astype(bf16)
                eaten = None
                for g in range(groups):
                    gain = pl.reciprocal(spread_s[0, r, g] * y + spread_s[1, r, g], approx=True)
                    growth[g] = growth[g] + gain
                    short = gain.astype(bf16)
                    taken = short * scale
                    flux[g] = taken if r == 0 else flux[g] + taken
                    part = short * mass_s[g * GROUP : (g + 1) * GROUP, lanes]
                    eaten = part if g == 0 else eaten + part
                eaten_s[r0 + r, :, lanes] = eaten
            for g in range(groups):
                strains = slice(g * GROUP, (g + 1) * GROUP)
                growth_ref[strains, lanes] = growth[g]
                flux_ref[strains, lanes] += flux[g].astype(f32)
            return 0

        lax.fori_loop(0, tiles, per_tile, 0, unroll=4)
        return 0

    lax.fori_loop(0, blocks, per_block, 0)
    sum_block(blocks - 1)


def copy_mass(mass_ref, mass_s):
    mass_s[...] = mass_ref[...].astype(f32).astype(bf16)


def first_kernel(row0, parts, *refs):
    seen = refs[:parts]
    coefficients, mass_ref = refs[parts : parts + 4], refs[parts + 4]
    growth_ref, flux_ref, consumed_ref = refs[parts + 5 : parts + 8]
    mass_s, *work = refs[parts + 8 :]
    copy_mass(mass_ref, mass_s)
    growth_ref[...] = jnp.zeros_like(growth_ref)
    flux_ref[...] = jnp.zeros_like(flux_ref)
    uptake_sums(row0, seen, *coefficients, mass_s, growth_ref, flux_ref, consumed_ref, *work)


def finish(first_ref, flux_ref, mass_ref, secretion_ref, consumed_refs, net_refs):
    cells = flux_ref.shape[1]
    resources = secretion_ref.shape[0]
    turn = lax.rem(resources - first_ref[0], resources)
    secretion = pltpu.roll(secretion_ref[...].astype(f32), turn, 0).astype(bf16)
    base = None
    for tile in range(cells // WIDE):
        lanes = slice(tile * WIDE, (tile + 1) * WIDE)
        product = (mass_ref[:, lanes].astype(f32) * flux_ref[:, lanes]).astype(bf16)
        secreted = jnp.dot(secretion, product, preferred_element_type=f32)
        consumed = [ref[:, lanes] for ref in consumed_refs]
        net = secreted - (consumed[0] if len(consumed) == 1 else jnp.concatenate(consumed, axis=0))
        if base is None:
            base = jnp.mean(net, axis=1, keepdims=True).astype(bf16).astype(f32)
            base = jnp.broadcast_to(base, (net.shape[0], LANES))
        start = 0
        for ref in net_refs:
            rows = slice(start, start + ref.shape[0])
            start += ref.shape[0]
            if ref.dtype == f32:
                ref[:, lanes] = net[rows]
                continue
            ref[:, lanes] = (net[rows] - base[rows, :1]).astype(bf16)
            if tile == 0:
                ref[:, cells : cells + LANES] = base[rows].astype(bf16)


def second_kernel(row0, parts, owners, *refs):
    seen = refs[:parts]
    coefficients, mass_ref = refs[parts : parts + 4], refs[parts + 4]
    growth_in, flux_in, consumed_in, secretion_ref = refs[parts + 5 : parts + 9]
    growth_ref = refs[parts + 9]
    net_refs = refs[parts + 10 : parts + 10 + owners]
    flux_s, consumed_s, mass_s, *work = refs[parts + 10 + owners :]
    copy_mass(mass_ref, mass_s)
    growth_ref[...] = growth_in[...]
    flux_s[...] = flux_in[...]
    uptake_sums(row0, seen, *coefficients, mass_s, growth_ref, flux_s, consumed_s, *work)
    finish(coefficients[0], flux_s, mass_ref, secretion_ref, (consumed_in, consumed_s), net_refs)


def only_kernel(row0, parts, owners, *refs):
    seen = refs[:parts]
    coefficients, mass_ref, secretion_ref = refs[parts : parts + 4], refs[parts + 4], refs[parts + 5]
    growth_ref = refs[parts + 6]
    net_refs = refs[parts + 7 : parts + 7 + owners]
    flux_s, consumed_s, mass_s, *work = refs[parts + 7 + owners :]
    copy_mass(mass_ref, mass_s)
    growth_ref[...] = jnp.zeros_like(growth_ref)
    flux_s[...] = jnp.zeros_like(flux_s)
    uptake_sums(row0, seen, *coefficients, mass_s, growth_ref, flux_s, consumed_s, *work)
    finish(coefficients[0], flux_s, mass_ref, secretion_ref, (consumed_s,), net_refs)


def work_space(rows, strains, cells, resources):
    groups = strains // GROUP
    return [
        pltpu.VMEM((strains, cells), bf16),
        pltpu.VMEM((rows, cells), f32),
        pltpu.VMEM((strains, resources), f32),
        pltpu.VMEM((strains, resources), f32),
        pltpu.VMEM((rows, LANES), f32),
        pltpu.VMEM((2, GROUP, groups, GROUP, LANES), f32),
        pltpu.VMEM((rows, GROUP, cells), bf16),
    ]


def exchange(own, others, coefficients, mass, secretion, edges):
    strains, cells = mass.shape
    held = own.shape[0]
    total = coefficients[1].shape[1]
    sums = jax.ShapeDtypeStruct((strains, cells), f32)
    nets = tuple(
        jax.ShapeDtypeStruct((held, cells) if i == 0 else (held, cells + LANES), f32 if i == 0 else bf16)
        for i in range(total // held)
    )
    given = [pl.BlockSpec(memory_space=pltpu.SMEM)] + [whole()] * 4
    if held % GROUP:
        seen = jnp.concatenate([own] + others, axis=0)
        outs = pl.pallas_call(
            functools.partial(only_kernel, 0, 1, len(nets)),
            out_shape=(sums,) + nets,
            in_specs=[whole()] + given + [whole()],
            out_specs=(whole(),) * (1 + len(nets)),
            scratch_shapes=[pltpu.VMEM((strains, cells), f32), pltpu.VMEM((total, cells), f32)]
            + work_space(total, strains, cells, total),
            compiler_params=params(28),
            cost_estimate=estimate(total * strains * cells),
        )(seen, *coefficients, mass, secretion)
        return *halo(edges, "space"), outs[0], outs[1:]
    growth, flux, consumed = pl.pallas_call(
        functools.partial(first_kernel, 0, 1),
        out_shape=(sums, sums, jax.ShapeDtypeStruct((held, cells), f32)),
        in_specs=[whole()] + given,
        out_specs=(whole(),) * 3,
        scratch_shapes=work_space(held, strains, cells, total),
        compiler_params=params(28),
        cost_estimate=estimate(held * strains * cells),
    )(own, *coefficients, mass)
    edges, consumed = lax.optimization_barrier((edges, consumed))
    low, high = halo(edges, "space")
    rest = total - held
    outs = pl.pallas_call(
        functools.partial(second_kernel, held, len(others), len(nets)),
        out_shape=(sums,) + nets,
        in_specs=[whole()] * len(others) + given + [whole()] * 4,
        out_specs=(whole(),) * (1 + len(nets)),
        scratch_shapes=[pltpu.VMEM((strains, cells), f32), pltpu.VMEM((rest, cells), f32)]
        + work_space(rest, strains, cells, total),
        compiler_params=params(28),
        cost_estimate=estimate(rest * strains * cells),
    )(*others, *coefficients, mass, growth, flux, consumed, secretion)
    return low, high, outs[0], outs[1:]


def laplace(field, low, high, planes, plane):
    cell = lax.broadcasted_iota(jnp.int32, (field[0].shape[0], plane), 1)
    z = lax.rem(cell, NZ)
    out = []
    for x in range(planes):
        v = field[x]
        beside = (low if x == 0 else field[x - 1]) + (high if x == planes - 1 else field[x + 1])
        beside += jnp.where(z == 0, v, pltpu.roll(v, 1, 1))
        beside += jnp.where(z == NZ - 1, v, pltpu.roll(v, plane - 1, 1))
        beside += jnp.where(cell < NZ, v, pltpu.roll(v, NZ, 1))
        beside += jnp.where(cell >= plane - NZ, v, pltpu.roll(v, plane - NZ, 1))
        out.append(beside - 6.0 * v)
    return out


def planes_of(ref, rows, planes, plane):
    return [ref[rows, x * plane : (x + 1) * plane].astype(f32) for x in range(planes)]


def step_kernel(planes, plane, mass_ref, field_ref, low_ref, high_ref, sum_ref, net_ref, maintenance_ref,
                motility_ref, diffusivity_ref, supply_ref, growth_ref, new_ref, partial_ref, traits_s):
    strains = mass_ref.shape[0]
    held = field_ref.shape[0]
    traits_s[:, 0:1] = column(maintenance_ref[...])
    traits_s[:, 1:2] = column(motility_ref[...])

    def per_group(group, _):
        rows = pl.ds(pl.multiple_of(group * GROUP, GROUP), GROUP)
        mass = planes_of(mass_ref, rows, planes, plane)
        spread = laplace(mass, low_ref[rows, :].astype(f32), high_ref[rows, :].astype(f32), planes, plane)
        maintenance = traits_s[rows, 0:1]
        motility = traits_s[rows, 1:2]
        for x in range(planes):
            growth = sum_ref[rows, x * plane : (x + 1) * plane] - maintenance
            growth_ref[rows, x, :] = growth
            new_ref[rows, x, :] = mass[x] + time_step * (mass[x] * growth + motility * spread[x])
        return 0

    lax.fori_loop(0, strains // GROUP, per_group, 0)
    field = planes_of(field_ref, slice(0, held), planes, plane)
    beyond = slice(strains, strains + held)
    spread = laplace(field, low_ref[beyond, :].astype(f32), high_ref[beyond, :].astype(f32), planes, plane)
    diffusivity = column(diffusivity_ref[...])
    supply = column(supply_ref[...])
    for x in range(planes):
        lanes = slice(x * plane, (x + 1) * plane)
        change = diffusivity * spread[x] + net_ref[:, lanes] + supply
        partial_ref[:, lanes] = field[x] + time_step * change


def halo(block, axis):
    count = lax.axis_size(axis)
    forward = [(i, (i + 1) % count) for i in range(count)]
    backward = [(target, source) for source, target in forward]
    low = lax.ppermute(block[:, -1, :], axis, forward)
    high = lax.ppermute(block[:, 0, :], axis, backward)
    return low, high


def shifted(value, axis, shift):
    count = lax.axis_size(axis)
    return lax.ppermute(value, axis, [(i, (i + shift) % count) for i in range(count)])


def per_device(
    biomass,
    resources,
    capacity,
    affinity,
    secretion,
    energy_yield,
    maintenance,
    motility,
    diffusivity,
    supply,
):
    strains, slab_rows, plane = biomass.shape
    cells = slab_rows * plane
    held = resources.shape[0]
    count = lax.axis_size("species")
    total = held * count
    field = resources.reshape(held, cells)
    own = field.astype(bf16)
    others = [shifted(own, "species", -j) for j in range(1, count)]
    mass = biomass.reshape(strains, cells)
    first = lax.axis_index("species") * held
    coefficients = (first[None].astype(jnp.int32), capacity, affinity, energy_yield[None, :])
    edges = jnp.concatenate([biomass, resources.astype(bf16)], axis=0)
    low, high, gained, nets = exchange(own, others, coefficients, mass, secretion, edges)
    arrived = [shifted(nets[j], "species", j) for j in range(1, count)]
    sums = jax.ShapeDtypeStruct(biomass.shape, f32)
    growth, new_biomass, partial = pl.pallas_call(
        functools.partial(step_kernel, slab_rows, plane),
        out_shape=(sums, sums, jax.ShapeDtypeStruct((held, cells), f32)),
        in_specs=[whole()] * 10,
        out_specs=(whole(),) * 3,
        scratch_shapes=[pltpu.VMEM((strains, LANES), f32)],
        compiler_params=params(28),
        cost_estimate=estimate(strains * cells * 8),
    )(mass, field, low, high, gained, nets[0], maintenance[None, :], motility[None, :],
      diffusivity[None, :], supply[None, :])
    arrived, partial = lax.optimization_barrier((arrived, partial))
    received = sum(part[:, :cells].astype(f32) for part in arrived)
    base = sum(part[:, cells:].astype(f32) for part in arrived)
    received = received + jnp.concatenate([base] * (cells // LANES), axis=1)
    new_resources = (partial + time_step * received).reshape(resources.shape)
    return growth, new_biomass, new_resources


def solution(mesh):
    return jax.shard_map(
        per_device,
        mesh=mesh,
        in_specs=(
            P("species", "space", None),
            P("species", "space", None),
            P("species", None),
            P("species", None),
            P(None, "species"),
            P(),
            P("species"),
            P("species"),
            P("species"),
            P("species"),
        ),
        out_specs=(
            P("species", "space", None),
            P("species", "space", None),
            P("species", "space", None),
        ),
        check_vma=False,
    )
```

```python
import functools

import jax
import jax.numpy as jnp
from jax import lax
from jax.experimental import pallas as pl
from jax.experimental.pallas import tpu as pltpu
from jax.sharding import PartitionSpec as P

NY = 16
NZ = 64

time_step = 0.25

bf16 = jnp.bfloat16
f32 = jnp.float32
LANES = 128
GROUP = 16
WIDE = 256


def whole():
    return pl.BlockSpec(memory_space=pltpu.VMEM)


def params(limit):
    return pltpu.CompilerParams(vmem_limit_bytes=limit << 20)


def estimate(elements):
    return pl.CostEstimate(flops=40 * elements, bytes_accessed=1 << 20, transcendentals=elements)


def column(row):
    size = row.shape[1]
    shape = (size, size)
    own = lax.broadcasted_iota(jnp.int32, shape, 0) == lax.broadcasted_iota(jnp.int32, shape, 1)
    return jnp.sum(jnp.where(own, jnp.broadcast_to(row, shape), 0.0), axis=1, keepdims=True)


def uptake_sums(row0, seen_refs, first_ref, capacity_ref, affinity_ref, yield_ref, mass_s, growth_ref,
                flux_ref, consumed_ref, y_s, slopes_s, levels_s, inverse_s, spread_s, eaten_s):
    rows, cells = y_s.shape
    strains, resources = capacity_ref.shape
    groups = strains // GROUP
    blocks = rows // GROUP
    tiles = cells // LANES
    start = 0
    eaten_s[0:GROUP] = jnp.zeros_like(eaten_s[0:GROUP])
    for ref in seen_refs:
        count = ref.shape[0]
        y_s[start : start + count, :] = 1.0 / ref[...].astype(f32)
        start += count
    turn = lax.rem(2 * resources - first_ref[0] - row0, resources)
    level = 1.0 / (capacity_ref[...] * yield_ref[...])
    slopes_s[...] = pltpu.roll(affinity_ref[...] * level, turn, 1)
    levels_s[...] = pltpu.roll(level, turn, 1)
    inverse_s[...] = jnp.broadcast_to(1.0 / column(pltpu.roll(yield_ref[...], turn, 1))[:rows], inverse_s.shape)

    shape = (GROUP, GROUP * GROUP)
    ones = lax.broadcasted_iota(jnp.int32, shape, 1) // GROUP
    ones = (ones == lax.broadcasted_iota(jnp.int32, shape, 0)).astype(f32).astype(bf16)

    def sum_block(block):
        part = pl.ds(pl.multiple_of(block * GROUP, GROUP), GROUP)
        inverse = inverse_s[part, :1]
        for tile in range(cells // WIDE):
            lanes = slice(tile * WIDE, (tile + 1) * WIDE)
            eaten = eaten_s[part, :, lanes].reshape(GROUP * GROUP, WIDE)
            consumed_ref[part, lanes] = jnp.dot(ones, eaten, preferred_element_type=f32) * inverse

    def per_block(block, _):
        r0 = pl.multiple_of(block * GROUP, GROUP)
        for r in range(GROUP):
            chosen = jnp.full((GROUP, LANES), r0 + r, jnp.int32)
            for g in range(groups):
                members = slice(g * GROUP, (g + 1) * GROUP)
                spread_s[0, r, g] = jnp.take_along_axis(slopes_s[members, :], chosen, axis=1)
                spread_s[1, r, g] = jnp.take_along_axis(levels_s[members, :], chosen, axis=1)

        sum_block(jnp.maximum(block - 1, 0))

        def per_tile(tile, _):
            lanes = pl.ds(pl.multiple_of(tile * LANES, LANES), LANES)
            y_rows = y_s[pl.ds(r0, GROUP), lanes]
            inverse = inverse_s[pl.ds(r0, GROUP), :]
            growth = [growth_ref[g * GROUP : (g + 1) * GROUP, lanes] for g in range(groups)]
            flux = [None] * groups
            for r in range(GROUP):
                y = jnp.broadcast_to(y_rows[r : r + 1], (GROUP, LANES))
                scale = jnp.broadcast_to(inverse[r : r + 1], (GROUP, LANES)).astype(bf16)
                eaten = None
                for g in range(groups):
                    gain = pl.reciprocal(spread_s[0, r, g] * y + spread_s[1, r, g], approx=True)
                    growth[g] = growth[g] + gain
                    short = gain.astype(bf16)
                    taken = short * scale
                    flux[g] = taken if r == 0 else flux[g] + taken
                    part = short * mass_s[g * GROUP : (g + 1) * GROUP, lanes]
                    eaten = part if g == 0 else eaten + part
                eaten_s[r0 + r, :, lanes] = eaten
            for g in range(groups):
                strains = slice(g * GROUP, (g + 1) * GROUP)
                growth_ref[strains, lanes] = growth[g]
                flux_ref[strains, lanes] += flux[g].astype(f32)
            return 0

        lax.fori_loop(0, tiles, per_tile, 0, unroll=4)
        return 0

    lax.fori_loop(0, blocks, per_block, 0)
    sum_block(blocks - 1)


def copy_mass(mass_ref, mass_s):
    mass_s[...] = mass_ref[...].astype(f32).astype(bf16)


def first_kernel(row0, parts, *refs):
    seen = refs[:parts]
    coefficients, mass_ref = refs[parts : parts + 4], refs[parts + 4]
    growth_ref, flux_ref, consumed_ref = refs[parts + 5 : parts + 8]
    mass_s, *work = refs[parts + 8 :]
    copy_mass(mass_ref, mass_s)
    growth_ref[...] = jnp.zeros_like(growth_ref)
    flux_ref[...] = jnp.zeros_like(flux_ref)
    uptake_sums(row0, seen, *coefficients, mass_s, growth_ref, flux_ref, consumed_ref, *work)


def finish(first_ref, flux_ref, mass_ref, secretion_ref, consumed_refs, net_refs):
    cells = flux_ref.shape[1]
    resources = secretion_ref.shape[0]
    turn = lax.rem(resources - first_ref[0], resources)
    secretion = pltpu.roll(secretion_ref[...].astype(f32), turn, 0).astype(bf16)
    base = None
    for tile in range(cells // WIDE):
        lanes = slice(tile * WIDE, (tile + 1) * WIDE)
        product = (mass_ref[:, lanes].astype(f32) * flux_ref[:, lanes]).astype(bf16)
        secreted = jnp.dot(secretion, product, preferred_element_type=f32)
        consumed = [ref[:, lanes] for ref in consumed_refs]
        net = secreted - (consumed[0] if len(consumed) == 1 else jnp.concatenate(consumed, axis=0))
        if base is None:
            base = jnp.mean(net, axis=1, keepdims=True).astype(bf16).astype(f32)
            base = jnp.broadcast_to(base, (net.shape[0], LANES))
        start = 0
        for ref in net_refs:
            rows = slice(start, start + ref.shape[0])
            start += ref.shape[0]
            if ref.dtype == f32:
                ref[:, lanes] = net[rows]
                continue
            ref[:, lanes] = (net[rows] - base[rows, :1]).astype(bf16)
            if tile == 0:
                ref[:, cells : cells + LANES] = base[rows].astype(bf16)


def second_kernel(row0, parts, owners, *refs):
    seen = refs[:parts]
    coefficients, mass_ref = refs[parts : parts + 4], refs[parts + 4]
    growth_in, flux_in, consumed_in, secretion_ref = refs[parts + 5 : parts + 9]
    growth_ref = refs[parts + 9]
    net_refs = refs[parts + 10 : parts + 10 + owners]
    flux_s, consumed_s, mass_s, *work = refs[parts + 10 + owners :]
    copy_mass(mass_ref, mass_s)
    growth_ref[...] = growth_in[...]
    flux_s[...] = flux_in[...]
    uptake_sums(row0, seen, *coefficients, mass_s, growth_ref, flux_s, consumed_s, *work)
    finish(coefficients[0], flux_s, mass_ref, secretion_ref, (consumed_in, consumed_s), net_refs)


def only_kernel(row0, parts, owners, *refs):
    seen = refs[:parts]
    coefficients, mass_ref, secretion_ref = refs[parts : parts + 4], refs[parts + 4], refs[parts + 5]
    growth_ref = refs[parts + 6]
    net_refs = refs[parts + 7 : parts + 7 + owners]
    flux_s, consumed_s, mass_s, *work = refs[parts + 7 + owners :]
    copy_mass(mass_ref, mass_s)
    growth_ref[...] = jnp.zeros_like(growth_ref)
    flux_s[...] = jnp.zeros_like(flux_s)
    uptake_sums(row0, seen, *coefficients, mass_s, growth_ref, flux_s, consumed_s, *work)
    finish(coefficients[0], flux_s, mass_ref, secretion_ref, (consumed_s,), net_refs)


def work_space(rows, strains, cells, resources):
    groups = strains // GROUP
    return [
        pltpu.VMEM((strains, cells), bf16),
        pltpu.VMEM((rows, cells), f32),
        pltpu.VMEM((strains, resources), f32),
        pltpu.VMEM((strains, resources), f32),
        pltpu.VMEM((rows, LANES), f32),
        pltpu.VMEM((2, GROUP, groups, GROUP, LANES), f32),
        pltpu.VMEM((rows, GROUP, cells), bf16),
    ]


def exchange(own, others, coefficients, mass, secretion, edges):
    strains, cells = mass.shape
    held = own.shape[0]
    total = coefficients[1].shape[1]
    sums = jax.ShapeDtypeStruct((strains, cells), f32)
    nets = tuple(
        jax.ShapeDtypeStruct((held, cells) if i == 0 else (held, cells + LANES), f32 if i == 0 else bf16)
        for i in range(total // held)
    )
    given = [pl.BlockSpec(memory_space=pltpu.SMEM)] + [whole()] * 4
    if held % GROUP:
        seen = jnp.concatenate([own] + others, axis=0)
        outs = pl.pallas_call(
            functools.partial(only_kernel, 0, 1, len(nets)),
            out_shape=(sums,) + nets,
            in_specs=[whole()] + given + [whole()],
            out_specs=(whole(),) * (1 + len(nets)),
            scratch_shapes=[pltpu.VMEM((strains, cells), f32), pltpu.VMEM((total, cells), f32)]
            + work_space(total, strains, cells, total),
            compiler_params=params(28),
            cost_estimate=estimate(total * strains * cells),
        )(seen, *coefficients, mass, secretion)
        return *halo(edges, "space"), outs[0], outs[1:]
    growth, flux, consumed = pl.pallas_call(
        functools.partial(first_kernel, 0, 1),
        out_shape=(sums, sums, jax.ShapeDtypeStruct((held, cells), f32)),
        in_specs=[whole()] + given,
        out_specs=(whole(),) * 3,
        scratch_shapes=work_space(held, strains, cells, total),
        compiler_params=params(28),
        cost_estimate=estimate(held * strains * cells),
    )(own, *coefficients, mass)
    edges, consumed = lax.optimization_barrier((edges, consumed))
    low, high = halo(edges, "space")
    rest = total - held
    outs = pl.pallas_call(
        functools.partial(second_kernel, held, len(others), len(nets)),
        out_shape=(sums,) + nets,
        in_specs=[whole()] * len(others) + given + [whole()] * 4,
        out_specs=(whole(),) * (1 + len(nets)),
        scratch_shapes=[pltpu.VMEM((strains, cells), f32), pltpu.VMEM((rest, cells), f32)]
        + work_space(rest, strains, cells, total),
        compiler_params=params(28),
        cost_estimate=estimate(rest * strains * cells),
    )(*others, *coefficients, mass, growth, flux, consumed, secretion)
    return low, high, outs[0], outs[1:]


def laplace(field, low, high, planes, plane):
    cell = lax.broadcasted_iota(jnp.int32, (field[0].shape[0], plane), 1)
    z = lax.rem(cell, NZ)
    out = []
    for x in range(planes):
        v = field[x]
        beside = (low if x == 0 else field[x - 1]) + (high if x == planes - 1 else field[x + 1])
        beside += jnp.where(z == 0, v, pltpu.roll(v, 1, 1))
        beside += jnp.where(z == NZ - 1, v, pltpu.roll(v, plane - 1, 1))
        beside += jnp.where(cell < NZ, v, pltpu.roll(v, NZ, 1))
        beside += jnp.where(cell >= plane - NZ, v, pltpu.roll(v, plane - NZ, 1))
        out.append(beside - 6.0 * v)
    return out


def planes_of(ref, rows, planes, plane):
    return [ref[rows, x * plane : (x + 1) * plane].astype(f32) for x in range(planes)]


def step_kernel(planes, plane, mass_ref, field_ref, low_ref, high_ref, sum_ref, net_ref, maintenance_ref,
                motility_ref, diffusivity_ref, supply_ref, growth_ref, new_ref, partial_ref, traits_s):
    strains = mass_ref.shape[0]
    held = field_ref.shape[0]
    traits_s[:, 0:1] = column(maintenance_ref[...])
    traits_s[:, 1:2] = column(motility_ref[...])

    def per_group(group, _):
        rows = pl.ds(pl.multiple_of(group * GROUP, GROUP), GROUP)
        mass = planes_of(mass_ref, rows, planes, plane)
        spread = laplace(mass, low_ref[rows, :].astype(f32), high_ref[rows, :].astype(f32), planes, plane)
        maintenance = traits_s[rows, 0:1]
        motility = traits_s[rows, 1:2]
        for x in range(planes):
            growth = sum_ref[rows, x * plane : (x + 1) * plane] - maintenance
            growth_ref[rows, x, :] = growth
            new_ref[rows, x, :] = mass[x] + time_step * (mass[x] * growth + motility * spread[x])
        return 0

    lax.fori_loop(0, strains // GROUP, per_group, 0)
    field = planes_of(field_ref, slice(0, held), planes, plane)
    beyond = slice(strains, strains + held)
    spread = laplace(field, low_ref[beyond, :].astype(f32), high_ref[beyond, :].astype(f32), planes, plane)
    diffusivity = column(diffusivity_ref[...])
    supply = column(supply_ref[...])
    for x in range(planes):
        lanes = slice(x * plane, (x + 1) * plane)
        change = diffusivity * spread[x] + net_ref[:, lanes] + supply
        partial_ref[:, lanes] = field[x] + time_step * change


def halo(block, axis):
    count = lax.axis_size(axis)
    forward = [(i, (i + 1) % count) for i in range(count)]
    backward = [(target, source) for source, target in forward]
    low = lax.ppermute(block[:, -1, :], axis, forward)
    high = lax.ppermute(block[:, 0, :], axis, backward)
    return low, high


def shifted(value, axis, shift):
    count = lax.axis_size(axis)
    return lax.ppermute(value, axis, [(i, (i + shift) % count) for i in range(count)])


def per_device(
    biomass,
    resources,
    capacity,
    affinity,
    secretion,
    energy_yield,
    maintenance,
    motility,
    diffusivity,
    supply,
):
    strains, slab_rows, plane = biomass.shape
    cells = slab_rows * plane
    held = resources.shape[0]
    count = lax.axis_size("species")
    total = held * count
    field = resources.reshape(held, cells)
    own = field.astype(bf16)
    others = [shifted(own, "species", -j) for j in range(1, count)]
    mass = biomass.reshape(strains, cells)
    first = lax.axis_index("species") * held
    coefficients = (first[None].astype(jnp.int32), capacity, affinity, energy_yield[None, :])
    edges = jnp.concatenate([biomass, resources.astype(bf16)], axis=0)
    low, high, gained, nets = exchange(own, others, coefficients, mass, secretion, edges)
    farthest = sorted(range(1, count), key=lambda j: -min(j, count - j))
    arrived = [shifted(nets[j], "species", j) for j in farthest]
    sums = jax.ShapeDtypeStruct(biomass.shape, f32)
    growth, new_biomass, partial = pl.pallas_call(
        functools.partial(step_kernel, slab_rows, plane),
        out_shape=(sums, sums, jax.ShapeDtypeStruct((held, cells), f32)),
        in_specs=[whole()] * 10,
        out_specs=(whole(),) * 3,
        scratch_shapes=[pltpu.VMEM((strains, LANES), f32)],
        compiler_params=params(28),
        cost_estimate=estimate(strains * cells * 8),
    )(mass, field, low, high, gained, nets[0], maintenance[None, :], motility[None, :],
      diffusivity[None, :], supply[None, :])
    arrived, partial = lax.optimization_barrier((arrived, partial))
    received = sum(part[:, :cells].astype(f32) for part in arrived)
    base = sum(part[:, cells:].astype(f32) for part in arrived)
    received = received + jnp.concatenate([base] * (cells // LANES), axis=1)
    new_resources = (partial + time_step * received).reshape(resources.shape)
    return growth, new_biomass, new_resources


def solution(mesh):
    return jax.shard_map(
        per_device,
        mesh=mesh,
        in_specs=(
            P("species", "space", None),
            P("species", "space", None),
            P("species", None),
            P("species", None),
            P(None, "species"),
            P(),
            P("species"),
            P("species"),
            P("species"),
            P("species"),
        ),
        out_specs=(
            P("species", "space", None),
            P("species", "space", None),
            P("species", "space", None),
        ),
        check_vma=False,
    )
```
